128 devices in a mesh: section: 2 (over y_lo), dp: 32 (over y_hi, z, x), tensor: 2 (over core).
Axes of the slice: x: 4, y: 4 (y_hi: 2, y_lo: 2; y = y_hi * 2 + y_lo), z: 4, core: 2. Of those that a mesh axis runs over, the one named last changes fastest.
Arguments:
- block_input: bfloat16 [2, 16384, 512], P(None, ('dp', 'tensor')), may hold values from -6 to 6
- out_cotangent: bfloat16 [2, 16384, 512], P(None, ('dp', 'tensor')), may hold values from -6 to 6
- segments: int32 [2, 16384], P(None, 'dp'), may hold values from 0 to 255, as said below
- positions: int32 [2, 16384], P(None, 'dp'), may hold values from 0 to 1535, as said below
- norm_gains: bfloat16 [2, 2, 512], P('section', None, ('dp', 'tensor')), may hold values from 0.099609375 to 1.8984375
- norm_shifts: bfloat16 [2, 2, 512], P('section', None, ('dp', 'tensor')), may hold values from -3 to 3
- inward_weight: bfloat16 [2, 512, 3, 512], P('section', 'dp', None, 'tensor'), may hold values from -0.25 to 0.25
- inward_bias: bfloat16 [2, 3, 8, 64], P('section', None, 'tensor', 'dp'), may hold values from -3 to 3
- outward_weight: bfloat16 [2, 512, 512], P('section', 'tensor', 'dp'), may hold values from -1 to 1
- outward_bias: bfloat16 [2, 512], P('section', ('dp', 'tensor')), may hold values from -3 to 3
- expand_weight: bfloat16 [2, 512, 2048], P('section', 'dp', 'tensor'), may hold values from -0.25 to 0.25
- expand_bias: bfloat16 [2, 16, 128], P('section', 'tensor', 'dp'), may hold values from -3 to 3
- shrink_weight: bfloat16 [2, 2048, 512], P('section', 'tensor', 'dp'), may hold values from -0.125 to 0.125
- shrink_bias: bfloat16 [2, 512], P('section', ('dp', 'tensor')), may hold values from -3 to 3
Outputs:
- hidden_states: bfloat16 [2, 2, 16384, 512], P('section', None, ('dp', 'tensor'))
- input_grads: float32 [2, 2, 16384, 512], P('section', None, ('dp', 'tensor'))
- gains_grad: float32 [2, 2, 512], P('section', None, ('dp', 'tensor'))
- shifts_grad: float32 [2, 2, 512], P('section', None, ('dp', 'tensor'))
- inward_weight_grad: float32 [2, 512, 3, 512], P('section', 'dp', None, 'tensor')
- inward_bias_grad: float32 [2, 3, 8, 64], P('section', None, 'tensor', 'dp')
- outward_weight_grad: float32 [2, 512, 512], P('section', 'tensor', 'dp')
- outward_bias_grad: float32 [2, 512], P('section', ('dp', 'tensor'))
- expand_weight_grad: float32 [2, 512, 2048], P('section', 'dp', 'tensor')
- expand_bias_grad: float32 [2, 16, 128], P('section', 'tensor', 'dp')
- shrink_weight_grad: float32 [2, 2048, 512], P('section', 'tensor', 'dp')
- shrink_bias_grad: float32 [2, 512], P('section', ('dp', 'tensor'))
The draws below stay inside these ranges and needn't reach their ends.
Inputs may be any that keep to these rules, and one draw needn't show every extreme that they name: `segments`: document numbers never fall along the tokens, and tokens of different packed sequences of 512 tokens have different numbers. Within a document the positions rise by one from token to token.
All inputs are finite; a program needn't handle non-finite values.
Results may differ from the reference program's by a relative error of at most 0.025.
Values may be sent and summed in bfloat16 or wider, within the bound.
A program may use at most 128 MiB of HBM per device.

```python
import jax
import jax.numpy as jnp
from jax import lax

D = 512
H = 8
HD = 64
FF = 2048
ROT = 16
LEN = 512
MICRO = 2
SECTIONS = 2
TOKENS = 16384


def document_cuts(key):
    seq_count = MICRO * TOKENS // LEN
    cut_second = jax.random.randint(jax.random.fold_in(key, 21), (seq_count, 1), 1, LEN // 4 + 1)
    cut_first = jax.random.randint(jax.random.fold_in(key, 22), (seq_count, 1), 1, cut_second + 1)
    cut_third = jax.random.randint(jax.random.fold_in(key, 23), (seq_count, 1), 3 * LEN // 4, LEN)
    anchor_any = jax.random.randint(jax.random.fold_in(key, 24), (seq_count, 1), 0, 1537 - cut_first)
    first_row = jnp.arange(seq_count, dtype=jnp.int32)[:, None] == 0
    anchor = jnp.where(first_row, 1536 - cut_first, anchor_any)
    places = jnp.arange(LEN, dtype=jnp.int32)[None, :]
    inside = (places >= cut_first).astype(jnp.int32) + (places >= cut_second).astype(jnp.int32) + (places >= cut_third).astype(jnp.int32)
    return (cut_first, cut_second, cut_third, anchor, places, inside)


def draw_segments(key, part):
    cut_first, cut_second, cut_third, anchor, places, inside = document_cuts(key)
    number = inside + 4 * jnp.arange(inside.shape[0], dtype=jnp.int32)[:, None]
    return number.reshape(MICRO, TOKENS).astype(jnp.int32)


def draw_positions(key, part):
    cut_first, cut_second, cut_third, anchor, places, inside = document_cuts(key)
    doc_start = jnp.where(inside == 0, -anchor, jnp.where(inside == 1, cut_first, jnp.where(inside == 2, cut_second, cut_third)))
    return (places - doc_start).reshape(MICRO, TOKENS).astype(jnp.int32)


def block_scale(own_key, dims, split, smallest, high):
    level, own = 1.0, jax.random.fold_in(own_key, 6)
    for axis_at, blocks in split:
        heights = jnp.exp(jax.random.uniform(jax.random.fold_in(own, axis_at), (blocks,), jnp.float32, smallest / len(split), high / len(split)))
        level = level * jnp.repeat(heights, dims[axis_at] // blocks).reshape([-1 if axis == axis_at else 1 for axis in range(len(dims))])
    return level


def noise(own_key, shape, width, bound, shards=(), held_as=jnp.bfloat16):
    level = block_scale(own_key, shape, shards, -0.22, 0.18) if shards else 1.0
    drawn = jax.random.normal(own_key, shape, jnp.float32) * width * level
    return jnp.minimum(jnp.maximum(drawn, -bound), bound).astype(held_as)


def setup_inputs(seed: int = 0) -> dict:
    key_of = jax.random.split(jax.random.key(seed), 15)
    return {
        "block_input": noise(key_of[0], (MICRO, TOKENS, D), 1.0, 6.0, ((1, 64),)),
        "out_cotangent": noise(key_of[1], (MICRO, TOKENS, D), 1.0, 6.0, ((1, 64),)),
        "segments": draw_segments(jax.random.fold_in(key_of[14], 71), 0),
        "positions": draw_positions(jax.random.fold_in(key_of[14], 71), 0),
        "norm_gains": jnp.clip(1.0 + 0.18 * jax.random.normal(key_of[4], (SECTIONS, 2, D), jnp.float32), 0.099609375, 1.8984375).astype(jnp.bfloat16),
        "norm_shifts": noise(key_of[5], (SECTIONS, 2, D), 0.5, 3.0, ((0, 2), (2, 64))),
        "inward_weight": noise(key_of[6], (SECTIONS, D, 3, D), D ** -0.5, 0.25, ((0, 2), (1, 32), (3, 2))),
        "inward_bias": noise(key_of[7], (SECTIONS, 3, H, HD), 0.5, 3.0, ((0, 2), (2, 2), (3, 32))),
        "outward_weight": noise(key_of[8], (SECTIONS, D, D), (D // 16) ** -0.5, 1.0, ((0, 2), (1, 2), (2, 32))),
        "outward_bias": noise(key_of[9], (SECTIONS, D), 0.5, 3.0, ((0, 2), (1, 64))),
        "expand_weight": noise(key_of[10], (SECTIONS, D, FF), D ** -0.5, 0.25, ((0, 2), (1, 32), (2, 2))),
        "expand_bias": noise(key_of[11], (SECTIONS, FF // 128, 128), 0.5, 3.0, ((0, 2), (1, 2), (2, 32))),
        "shrink_weight": noise(key_of[12], (SECTIONS, FF, D), FF ** -0.5, 0.125, ((0, 2), (1, 2), (2, 32))),
        "shrink_bias": noise(key_of[13], (SECTIONS, D), 0.5, 3.0, ((0, 2), (1, 64))),
    }


@jax.custom_vjp
def low(v):
    return lax.optimization_barrier(v.astype(jnp.bfloat16)).astype(jnp.float32)

@jax.custom_vjp
def low_back(v):
    return v

def low_keep(v):
    return (low(v), None)

def low_pass(kept, grad):
    return (grad,)

def back_keep(v):
    return (v, None)

def back_low(kept, grad):
    return (low(grad),)
low.defvjp(low_keep, low_pass)
low_back.defvjp(back_keep, back_low)
EPSILON = 1e-05
HIGHEST = lax.Precision.HIGHEST
MASKED = -1e+30

def norm_rows(values, gain, shift):
    center = values - lax.optimization_barrier(jnp.mean(values, axis=-1, keepdims=True))
    spread = lax.optimization_barrier(jnp.mean(center * center, axis=-1, keepdims=True))
    return center * lax.rsqrt(spread + EPSILON) * gain + shift

def turning(places):
    steps_half = jnp.arange(ROT // 2).astype(jnp.float32)
    rates = 10000.0 ** (-2.0 * steps_half / ROT)
    angles = places.astype(jnp.float32)[:, None] * rates[None, :]
    return (jnp.cos(angles)[:, None, :], jnp.sin(angles)[:, None, :])

def rotate(values, cosine, sine_part):
    half_rot = ROT // 2
    front = values[..., :half_rot]
    behind = values[..., half_rot:ROT]
    return jnp.concatenate([front * cosine - behind * sine_part, behind * cosine + front * sine_part, values[..., ROT:]], axis=-1)

def allowed_pairs(labels):
    places = jnp.arange(LEN)
    return (labels[:, None] == labels[None, :]) & (places[None, :] <= places[:, None])

def attend(block_args):
    queries, keys_rot, values, labels = block_args
    scores = jnp.einsum('qhd,khd->hqk', queries, keys_rot, precision=HIGHEST) * HD ** (-0.5)
    scores = low_back(scores)
    scores = jnp.where(allowed_pairs(labels)[None], scores, MASKED)
    row_max = lax.optimization_barrier(jnp.max(scores, axis=-1, keepdims=True))
    powers = jnp.exp(scores - row_max)
    shares = low(powers / lax.optimization_barrier(jnp.sum(powers, axis=-1, keepdims=True)))
    return jnp.einsum('hqk,khd->qhd', shares, values, precision=HIGHEST)

def apply_layer(inputs, params, places, labels):
    gains, shifts, inward_weight, inward_bias, outward_weight, outward_bias, expand_weight, expand_bias, shrink_weight, shrink_bias = params
    first = low(norm_rows(inputs, gains[0], shifts[0]))
    second = low(norm_rows(inputs, gains[1], shifts[1]))
    joint = jnp.dot(first, inward_weight.reshape(D, 3 * D), precision=HIGHEST) + inward_bias.reshape(3 * D)
    joint = low_back(joint).reshape(-1, 3, H, HD)
    cosine, sine_part = turning(places)
    queries = low(rotate(joint[:, 0], cosine, sine_part))
    keys_rot = low(rotate(joint[:, 1], cosine, sine_part))
    values = low(joint[:, 2])
    shape_seq = (-1, LEN, H, HD)
    mixed = lax.map(jax.checkpoint(attend), (queries.reshape(shape_seq), keys_rot.reshape(shape_seq), values.reshape(shape_seq), labels.reshape(-1, LEN)))
    mixed = low(low_back(mixed.reshape(-1, D)))
    before = low_back(jnp.dot(second, expand_weight, precision=HIGHEST) + expand_bias.reshape(FF))
    hidden = low(jax.nn.gelu(before, approximate=False))
    branch = jnp.dot(mixed, outward_weight, precision=HIGHEST) + jnp.dot(hidden, shrink_weight, precision=HIGHEST)
    return inputs + low_back(branch) + outward_bias + shrink_bias

def reference(block_input, out_cotangent, segments, positions, norm_gains, norm_shifts, inward_weight, inward_bias, outward_weight, outward_bias, expand_weight, expand_bias, shrink_weight, shrink_bias):
    params = tuple((member.astype(jnp.float32) for member in (norm_gains, norm_shifts, inward_weight, inward_bias, outward_weight, outward_bias, expand_weight, expand_bias, shrink_weight, shrink_bias)))
    start_rows = block_input.astype(jnp.float32)
    bump_rows = jnp.zeros((SECTIONS - 1,) + block_input.shape, jnp.float32)

    def run(params, start_rows, bump_rows):
        finals = []
        layers_out = []
        for batch_index in range(MICRO):
            current = start_rows[batch_index]
            per_section = []
            for section_index in range(SECTIONS):
                if section_index > 0:
                    current = low_back(low(current)) + bump_rows[section_index - 1, batch_index]
                current = apply_layer(current, tuple((member[section_index] for member in params)), positions[batch_index], segments[batch_index])
                per_section.append(current)
            finals.append(current)
            layers_out.append(jnp.stack(per_section))
        return (jnp.stack(finals), jnp.stack(layers_out, axis=1))
    finals, pullback, layers_out = jax.vjp(run, params, start_rows, bump_rows, has_aux=True)
    param_grads, grad_start, grad_bumps = pullback(out_cotangent.astype(jnp.float32))
    hidden_states = layers_out.astype(jnp.bfloat16)
    input_grads = jnp.concatenate([grad_start[None], grad_bumps], axis=0)
    return (hidden_states, input_grads, param_grads[0], param_grads[1], param_grads[2], param_grads[3], param_grads[4], param_grads[5], param_grads[6], param_grads[7], param_grads[8], param_grads[9])
```

```python
import jax
import jax.numpy as jnp
import numpy as np
from jax import lax
from jax.experimental import pallas as pl
from jax.experimental.pallas import tpu as pltpu
from jax.sharding import PartitionSpec as P

MESH = pl.DeviceIdType.MESH
BF = jnp.bfloat16
F32 = jnp.float32
HD = 64
ROT = 16
LEN = 512
D = 512
OWN = 256
HEADS = 4
EPSILON = 1e-05
MASKED = -1e30

COLS = 3200
IN, OUT, EXP, SHR, VEC = 0, 768, 1024, 2048, 3072
PARTS = ((0, 1024), (1024, 1024), (2048, 1152))
ORDERS = (("y", "z", "x"), ("z", "x", "y"), ("x", "y", "z"))
HALF = 512

V_IN, V_EXP, V_OUTB, V_SHRB, V_G0, V_G1, V_B0, V_B1, V_ALL = 0, 768, 1792, 2304, 2816, 3328, 3840, 4352, 4864


def where_am_i():
    s = lax.axis_index("section"); d = lax.axis_index("dp")
    return {"x": d % 4, "z": (d // 4) % 4, "y": (d // 16) * 2 + s}


def chip_id(c):
    return {"section": c["y"] % 2, "dp": (c["y"] // 2) * 16 + c["z"] * 4 + c["x"]}


def moved(c, axis, by):
    return {**c, axis: (c[axis] + by) % 4}


def slots(c, free, fixed_axis_val=None):
    full = slice(None)
    y = c["y"]
    return ((full, full) if "y" in free else (y % 2, y // 2)) + (
        full if "z" in free else c["z"], full if "x" in free else c["x"])


def region(ref, c, free, lo, width):
    return ref.at[slots(c, free) + (slice(None), pl.ds(lo, width))]


def greet(c):
    barrier = pltpu.get_barrier_semaphore()
    for axis in "xyz":
        for by in (1, -1):
            pl.semaphore_signal(barrier, inc=1, device_id=chip_id(moved(c, axis, by)), device_id_type=MESH)
    pl.semaphore_signal(barrier, inc=1, device_id={"tensor": 1 - lax.axis_index("tensor")}, device_id_type=MESH)
    pl.semaphore_wait(barrier, 7)


def push(src, dst, send, recv, target):
    return pltpu.make_async_remote_copy(src_ref=src, dst_ref=dst, send_sem=send, recv_sem=recv, device_id=target, device_id_type=MESH)


def gather(held, c, send, recv):
    for stage in range(3):
        first = []
        for p, (lo, width) in enumerate(PARTS):
            axis = ORDERS[p][stage]; done = ORDERS[p][:stage]
            own = region(held, c, done, lo, width)
            pair = []
            for k, by in enumerate((1, -1)):
                cp = push(own, own, send.at[p, stage, k], recv.at[p, stage, k], chip_id(moved(c, axis, by)))
                cp.start(); pair.append(cp)
            first.append(pair)
        second = []
        for p, (lo, width) in enumerate(PARTS):
            axis = ORDERS[p][stage]; done = ORDERS[p][:stage]
            pair = []
            for k, by in enumerate((1, -1)):
                src = moved(c, axis, -by)
                got = region(held, src, done, lo, width)
                push(got, got, send.at[p, stage, k], recv.at[p, stage, k], chip_id(src)).wait_recv()
                sub = (lo, HALF) if k == 0 else (lo + HALF, width - HALF)
                part = region(held, src, done, *sub)
                cp = push(part, part, send.at[p, stage, 2 + k], recv.at[p, stage, 2 + k], chip_id(moved(c, axis, by)))
                cp.start(); pair.append(cp)
            second.append(pair)
        for p, (lo, width) in enumerate(PARTS):
            axis = ORDERS[p][stage]; done = ORDERS[p][:stage]
            far = moved(c, axis, 2)
            for k in range(2):
                sub = (lo, HALF) if k == 0 else (lo + HALF, width - HALF)
                part = region(held, far, done, *sub)
                push(part, part, send.at[p, stage, 2 + k], recv.at[p, stage, 2 + k], chip_id(far)).wait_recv()
        for pair in first + second:
            for cp in pair:
                cp.wait_send()


def reduce_shapes(p, stage):
    lo, width = PARTS[p]
    order = ORDERS[p][::-1]
    pend = order[stage + 1:]
    lead = ((2, 2) if "y" in pend else ()) + ((4,) if "z" in pend else ()) + ((4,) if "x" in pend else ())
    return [lead + (16, HALF), lead + (16, width - HALF), lead + (16, width), lead + (16, width)]


def reduce_scratch():
    return [pltpu.VMEM(s, BF) for p in range(3) for st in range(3) for s in reduce_shapes(p, st)]


def accumulate(total, c, free, lo, width, others):
    dims = []
    for ax in "yzx":
        if ax in free:
            dims.append((ax, 4))
    n = 4 ** len(dims)

    def body(i, _):
        cc = dict(c); rest = i; lead = {}
        for ax, size in reversed(dims):
            cc[ax] = rest % 4; rest = rest // 4
        at = (cc["y"] % 2, cc["y"] // 2, cc["z"], cc["x"], slice(None), pl.ds(lo, width))
        oat = ()
        if "y" in free: oat += (cc["y"] % 2, cc["y"] // 2)
        if "z" in free: oat += (cc["z"],)
        if "x" in free: oat += (cc["x"],)
        v = total[at].astype(F32)
        for o in others:
            v = v + o[oat].astype(F32)
        total[at] = v.astype(BF)
        return 0
    if n == 1:
        body(0, 0)
    else:
        lax.fori_loop(0, n, body, 0)


def reduce(total, c, bufs, send, recv):
    buf = lambda p, st, k: bufs[(p * 3 + st) * 4 + k]
    for stage in range(3):
        first, second = [], []
        for p, (lo, width) in enumerate(PARTS):
            order = ORDERS[p][::-1]; axis = order[stage]; pend = order[stage + 1:]
            far = moved(c, axis, 2)
            for k, by in enumerate((1, -1)):
                sub = (lo, HALF) if k == 0 else (lo + HALF, width - HALF)
                cp = push(region(total, far, pend, *sub), buf(p, stage, k), send.at[p, stage, k], recv.at[p, stage, k], chip_id(moved(c, axis, by)))
                cp.start(); first.append(cp)
        for p, (lo, width) in enumerate(PARTS):
            order = ORDERS[p][::-1]; axis = order[stage]; pend = order[stage + 1:]
            for k, by in enumerate((1, -1)):
                sub = (lo, HALF) if k == 0 else (lo + HALF, width - HALF)
                first[2 * p + k].wait_recv()
                to = moved(c, axis, by)
                accumulate(total, to, pend, *sub, [buf(p, stage, k)])
                cp = push(region(total, to, pend, lo, width), buf(p, stage, 2 + k), send.at[p, stage, 2 + k], recv.at[p, stage, 2 + k], chip_id(to))
                cp.start(); second.append(cp)
        for p, (lo, width) in enumerate(PARTS):
            order = ORDERS[p][::-1]; axis = order[stage]; pend = order[stage + 1:]
            for k in range(2):
                second[2 * p + k].wait_recv()
            accumulate(total, c, pend, lo, width, [buf(p, stage, 2), buf(p, stage, 3)])
        for cp in first + second:
            cp.wait_send()


def dot(a, b):
    return jnp.dot(a, b, preferred_element_type=F32)


def dot_nt(a, b):
    return lax.dot_general(a, b, (((1,), (1,)), ((), ())), preferred_element_type=F32)


def weight(held, layer, lo, width):
    return held[layer, :, :, :, :, lo : lo + width].reshape(D, width)


def keep_grad(total, layer, lo, value):
    width = value.shape[-1]
    total[layer, :, :, :, :, lo : lo + width] = value.astype(BF).reshape(2, 4, 4, 16, width)


def vector_maps():
    at = lax.broadcasted_iota(jnp.int32, (1, V_ALL), 1)
    exp_at = at - V_EXP
    wide = at - V_OUTB
    wide_at = wide & 511
    is_in, is_exp = at < V_EXP, at < V_OUTB
    owner = jnp.where(is_in, (at & 63) >> 1, jnp.where(is_exp, (exp_at & 127) >> 2, wide_at >> 4))
    lane = jnp.where(
        is_in,
        ((at >> 6) << 1) + (at & 1),
        jnp.where(is_exp, 24 + ((exp_at >> 7) << 2) + (exp_at & 3), 56 + ((wide >> 9) << 3) + (wide_at & 7)),
    )
    core = (wide_at >> 3) & 1
    return owner, lane, core, is_exp


def decode_vectors(held, layer, me, table):
    owner, lane, core, is_exp = vector_maps()
    owners = lax.broadcasted_iota(jnp.int32, (32, V_ALL), 0)
    block = held[layer, :, :, :, :, VEC:COLS].reshape(32, 16, 128).astype(F32)
    result = jnp.zeros((1, V_ALL), F32)
    for row in range(2):
        spread = dot(block[:, row, :].astype(BF), table[...])
        wanted = jnp.where(jnp.where(is_exp, me, core) == row, owner, -1)
        result = result + jnp.sum(jnp.where(owners == wanted, spread, 0.0), axis=0, keepdims=True)
    return result


def encode_vectors(total, layer, me, table, vectors):
    owner, lane, core, is_exp = vector_maps()
    at = lax.broadcasted_iota(jnp.int32, (1, V_ALL), 1)
    owners = lax.broadcasted_iota(jnp.int32, (32, V_ALL), 0)
    rows = []
    for row in range(2):
        source = jnp.where(at < V_OUTB, me, jnp.where((at >= V_G0) | (core == me), core, 2))
        wanted = jnp.where(source == row, owner, -1)
        chosen = jnp.where(owners == wanted, vectors, 0.0).astype(BF)
        rows.append(dot_nt(chosen, table[...]))
    row_at = lax.broadcasted_iota(jnp.int32, (32, 16, 128), 1)
    block = jnp.where(row_at == 0, rows[0][:, None, :], jnp.where(row_at == 1, rows[1][:, None, :], 0.0))
    total[layer, :, :, :, :, VEC:COLS] = block.astype(BF).reshape(2, 4, 4, 16, 128)


def rolled(values, by):
    return pltpu.roll(values, by % values.shape[-1], 1)


def turned(values, cosine, sine_front, sine_back):
    return values * cosine + rolled(values, -(ROT // 2)) * sine_front + rolled(values, ROT // 2) * sine_back


def rows_of(i):
    return pl.ds(pl.multiple_of(i * OWN, OWN), OWN)


def forward(layer, r):
    held, vec = r.held, r.vec

    def project(i, carry):
        rows = rows_of(i)
        x = r.x[layer, rows, :].astype(F32)
        middle = jnp.mean(x, axis=-1, keepdims=True)
        center = x - middle
        scale = lax.rsqrt(jnp.mean(center * center, axis=-1, keepdims=True) + EPSILON)
        normal = center * scale
        r.moments[layer, 0, rows, :] = jnp.broadcast_to(middle, (OWN, 128))
        r.moments[layer, 1, rows, :] = jnp.broadcast_to(scale, (OWN, 128))
        first = (normal * vec[layer, :, V_G0:V_G1] + vec[layer, :, V_B0:V_B1]).astype(BF)
        second = (normal * vec[layer, :, V_G1:V_B0] + vec[layer, :, V_B1:V_ALL]).astype(BF)
        r.first_t[layer, :, rows] = first.T
        r.second_t[layer, :, rows] = second.T
        joint = dot(first, weight(held, layer, IN, 768)) + vec[layer, :, V_IN:V_EXP]
        cosine, front, back = [jnp.concatenate([r.angles[k, rows, :]] * 2, axis=1) for k in range(3)]
        query = turned(joint[:, :256], cosine, front, back).astype(BF) * BF(HD**-0.5)
        key = turned(joint[:, 256:512], cosine, front, back).astype(BF)
        value = joint[:, 512:].astype(BF)
        for k, part in enumerate((query, key, value)):
            part_t = part.T
            for h in range(HEADS):
                r.qkv[layer, k, h, rows, :] = part[:, h * HD : (h + 1) * HD]
                r.qkv_t[layer, k, h, :, rows] = part_t[h * HD : (h + 1) * HD]
        before = dot(second, weight(held, layer, EXP, 1024)) + vec[layer, :, V_EXP:V_OUTB]
        chance = 0.5 * (1.0 + lax.erf(before * (0.5**0.5)))
        r.hidden[layer, rows, :] = (before * chance).astype(BF)
        slope = chance + before * jnp.exp(-0.5 * before * before) * ((2.0 * np.pi) ** -0.5)
        r.slope[layer, rows, :] = slope.astype(BF)
        return carry

    lax.fori_loop(0, 2, project, 0)

    def attend(h, carry):
        for b in range(2):
            keys = (b + 1) * OWN
            cols = slice(b * OWN, keys)
            scores = dot(r.qkv[layer, 1, h, :keys, :], r.qkv_t[layer, 0, h, :, cols]) + r.mask[:keys, cols]
            powers = jnp.exp(scores - jnp.max(scores, axis=0, keepdims=True))
            shares = (powers * (1.0 / jnp.sum(powers, axis=0, keepdims=True))).astype(BF)
            r.shares[layer, h, :keys, cols] = shares
            r.mixed_t[layer, h, :, cols] = dot(r.qkv_t[layer, 2, h, :, :keys], shares)
        return carry

    lax.fori_loop(0, HEADS, attend, 0)
    r.mixed[layer] = r.mixed_t[layer].reshape(HEADS * HD, LEN).T.astype(BF)

    def close(i, carry):
        rows = rows_of(i)
        branch = dot_nt(r.mixed[layer, rows, :], weight(held, layer, OUT, 256))
        branch = branch + dot_nt(r.hidden[layer, rows, :], weight(held, layer, SHR, 1024))
        r.away[layer, rows, :] = branch.astype(BF)
        return carry

    lax.fori_loop(0, 2, close, 0)


def backward(layer, r):
    held, total, vec = r.held, r.total, r.vec

    def enter(i, carry):
        rows = rows_of(i)
        grad = r.grad[layer, rows, :]
        low = grad.astype(BF)
        r.grad_t[:, rows] = low.T
        mixed_grad = dot(low, weight(held, layer, OUT, 256)).astype(BF)
        mixed_grad_t = mixed_grad.T
        for h in range(HEADS):
            r.mixed_grad[h, rows, :] = mixed_grad[:, h * HD : (h + 1) * HD]
            r.mixed_grad_t[h, :, rows] = mixed_grad_t[h * HD : (h + 1) * HD]
        before = (dot(low, weight(held, layer, SHR, 1024)) * r.slope[layer, rows, :].astype(F32)).astype(BF)
        r.before_grad[rows, :] = before
        r.second_grad[rows, :] = dot_nt(before, weight(held, layer, EXP, 1024))
        return carry + jnp.sum(grad, axis=0, keepdims=True)

    out_sum = lax.fori_loop(0, 2, enter, jnp.zeros((1, D), F32))
    keep_grad(total, layer, OUT, dot(r.grad_t[...], r.mixed[layer]))
    for lo in range(0, 1024, 512):
        keep_grad(total, layer, SHR + lo, dot(r.grad_t[...], r.hidden[layer, :, lo : lo + 512]))
        keep_grad(total, layer, EXP + lo, dot(r.second_t[layer], r.before_grad[:, lo : lo + 512]))

    def attend(h, carry):
        key_parts, value_parts = [], []
        for b in range(2):
            keys = (b + 1) * OWN
            cols = slice(b * OWN, keys)
            shares = r.shares[layer, h, :keys, cols]
            out_t = r.mixed_grad_t[h, :, cols]
            delta = jnp.sum(out_t.astype(F32) * r.mixed_t[layer, h, :, cols], axis=0, keepdims=True)
            share_grad = dot(r.qkv[layer, 2, h, :keys, :], out_t)
            score_grad = (shares.astype(F32) * (share_grad - delta)).astype(BF)
            r.query_grad_t[h, :, cols] = dot(r.qkv_t[layer, 1, h, :, :keys], score_grad) * (HD**-0.5)
            key_parts.append(dot(score_grad, r.qkv[layer, 0, h, cols, :]))
            value_parts.append(dot(shares, r.mixed_grad[h, cols, :]))
        for k, parts in enumerate((key_parts, value_parts)):
            r.pair_grad[k, h, :OWN, :] = parts[0] + parts[1][:OWN]
            r.pair_grad[k, h, OWN:, :] = parts[1][OWN:]
        return carry

    lax.fori_loop(0, HEADS, attend, 0)

    def join(i, carry):
        rows = rows_of(i)
        cosine, front, back = [jnp.concatenate([r.angles[k, rows, :]] * 2, axis=1) for k in range(3)]
        query = r.query_grad_t[:, :, rows].reshape(HEADS * HD, OWN).T
        key = jnp.concatenate([r.pair_grad[0, h, rows, :] for h in range(HEADS)], axis=1)
        value = jnp.concatenate([r.pair_grad[1, h, rows, :] for h in range(HEADS)], axis=1)
        query = turned(query, cosine, -front, -back)
        key = turned(key, cosine, -front, -back)
        joint = jnp.concatenate([query, key, value], axis=1).astype(BF)
        r.joint_grad[rows, :] = joint
        first_grad = dot_nt(joint, weight(held, layer, IN, 768))
        second_grad = r.second_grad[rows, :]
        middle, scale = [jnp.concatenate([r.moments[layer, k, rows, :]] * 4, axis=1) for k in range(2)]
        normal = (r.x[layer, rows, :].astype(F32) - middle) * scale
        scaled = first_grad * vec[layer, :, V_G0:V_G1] + second_grad * vec[layer, :, V_G1:V_B0]
        passed = scaled - jnp.mean(scaled, axis=-1, keepdims=True)
        passed = passed - normal * jnp.mean(scaled * normal, axis=-1, keepdims=True)
        r.away[3 - layer, rows, :] = (passed * scale).astype(BF)
        sums = [joint.astype(F32), r.before_grad[rows, :].astype(F32), first_grad * normal, second_grad * normal, first_grad, second_grad]
        return tuple(c + jnp.sum(v, axis=0, keepdims=True) for c, v in zip(carry, sums))

    widths = (768, 1024, D, D, D, D)
    sums = lax.fori_loop(0, 2, join, tuple(jnp.zeros((1, w), F32) for w in widths))
    keep_grad(total, layer, IN, dot(r.first_t[layer], r.joint_grad[...]))
    vectors = jnp.concatenate([sums[0], sums[1], out_sum, out_sum, *sums[2:]], axis=1)
    encode_vectors(total, layer, r.me, r.table, vectors)


class Refs:
    pass


SCRATCH = dict(
    held=((2, 2, 4, 4, 16, COLS), BF),
    total=((2, 2, 4, 4, 16, COLS), BF),
    vec=((2, 1, V_ALL), F32),
    table=((128, V_ALL), BF),
    x=((2, LEN, D), BF),
    cot=((LEN, D), BF),
    grad=((2, LEN, D), F32),
    moments=((2, 2, LEN, 128), F32),
    first_t=((2, D, LEN), BF),
    second_t=((2, D, LEN), BF),
    qkv=((2, 3, HEADS, LEN, HD), BF),
    qkv_t=((2, 3, HEADS, HD, LEN), BF),
    shares=((2, HEADS, LEN, LEN), BF),
    mixed_t=((2, HEADS, HD, LEN), F32),
    mixed=((2, LEN, HEADS * HD), BF),
    hidden=((2, LEN, 1024), BF),
    slope=((2, LEN, 1024), BF),
    mask=((LEN, LEN), F32),
    away=((4, LEN, D), BF),
    come=((4, LEN, D), BF),
    grad_t=((D, LEN), BF),
    mixed_grad=((HEADS, LEN, HD), BF),
    mixed_grad_t=((HEADS, HD, LEN), BF),
    before_grad=((LEN, 1024), BF),
    second_grad=((LEN, D), F32),
    query_grad_t=((HEADS, HD, LEN), F32),
    pair_grad=((2, HEADS, LEN, HD), F32),
    joint_grad=((LEN, 768), BF),
    states=((2, OWN, D), BF),
    grads=((2, OWN, D), F32),
    grads_low=((2, OWN, D), BF),
    states_in=((OWN, D), BF),
    grads_in=((OWN, D), BF),
    small_in=((16, 128), BF),
    small_out=((16, 128), F32),
    small_back=((16, 128), F32),
)


def kernel(pack, x_in, cot_in, angles, seg_row, seg_col, states_out, grads_out, weights_out, vectors_out, *scratch):
    r = Refs()
    names = list(SCRATCH)
    for name, ref in zip(names, scratch):
        setattr(r, name, ref)
    gather_send, gather_recv, reduce_send, reduce_recv, near_send, near_recv, own_sem = scratch[len(names) : len(names) + 7]
    bufs = scratch[len(names) + 7 :]
    r.angles = angles
    c = where_am_i()
    section = lax.axis_index("section")
    me = r.me = lax.axis_index("tensor")
    other = {"tensor": 1 - me}
    mine = rows_of(me)

    def near(k, src, dst):
        return push(src, dst, near_send.at[k], near_recv.at[k], other)

    greet(c)
    small = near(0, pack.at[:, pl.ds(VEC, 128)], r.small_in)
    small.start()
    pairs = [near(1, x_in.at[section], r.x.at[0, mine]), near(2, cot_in.at[section], r.cot.at[mine])]
    owns = [
        pltpu.make_async_copy(x_in.at[section], r.x.at[0, mine], own_sem.at[0]),
        pltpu.make_async_copy(cot_in.at[section], r.cot.at[mine], own_sem.at[1]),
    ]
    for copy in pairs + owns:
        copy.start()
    held = r.held
    held[slots(c, ()) + (slice(None), slice(0, VEC))] = pack[:, :VEC]
    small.wait()
    both = pack[:, VEC:].astype(F32) + r.small_in[...].astype(F32)
    held[slots(c, ()) + (slice(None), slice(VEC, COLS))] = both.astype(BF)
    gather(held, c, gather_send, gather_recv)
    _, lane, _, _ = vector_maps()
    r.table[...] = (lax.broadcasted_iota(jnp.int32, (128, V_ALL), 0) == lane).astype(F32).astype(BF)
    for layer in range(2):
        r.vec[layer] = decode_vectors(held, layer, me, r.table)
    key_at = lax.broadcasted_iota(jnp.int32, (LEN, LEN), 0)
    query_at = lax.broadcasted_iota(jnp.int32, (LEN, LEN), 1)
    r.mask[...] = jnp.where((key_at <= query_at) & (seg_col[...] == seg_row[...]), 0.0, MASKED)
    for copy in pairs + owns:
        copy.wait()

    def swap(k):
        copy = near(3 + k, r.away.at[k], r.come.at[k])
        copy.start()
        copy.wait()

    for layer in range(2):
        forward(layer, r)
        swap(layer)
        bias = r.vec[layer, :, V_OUTB:V_SHRB] + r.vec[layer, :, V_SHRB:V_G0]

        def finish(rows):
            both = r.away[layer, rows, :].astype(F32) + r.come[layer, rows, :].astype(F32)
            return (r.x[layer, rows, :].astype(F32) + both + bias).astype(BF)

        if layer == 0:
            for i in range(2):
                rows = slice(i * OWN, (i + 1) * OWN)
                r.x[1, rows, :] = finish(rows)
        r.states[layer] = finish(mine)
    sides = [push(r.states.at[1 - section], r.states_in, near_send.at[8], near_recv.at[8], {"section": 1 - section})]
    sides[0].start()
    r.grad[1] = r.cot[...].astype(F32)
    for layer in (1, 0):
        backward(layer, r)
        swap(3 - layer)

        def pass_on(rows):
            both = r.away[3 - layer, rows, :].astype(F32) + r.come[3 - layer, rows, :].astype(F32)
            return r.grad[layer, rows, :] + both

        if layer == 1:
            for i in range(2):
                rows = slice(i * OWN, (i + 1) * OWN)
                r.grad[0, rows, :] = pass_on(rows).astype(BF).astype(F32)
        last = pass_on(mine)
        r.grads[layer] = last
        r.grads_low[layer] = last.astype(BF)
    sides.append(push(r.grads_low.at[1 - section], r.grads_in, near_send.at[9], near_recv.at[9], {"section": 1 - section}))
    sides[1].start()
    reduce(r.total, c, bufs, reduce_send, reduce_recv)
    own = r.total[slots(c, ())].astype(F32)
    weights_out[...] = own[:, :VEC]
    r.small_out[...] = own[:, VEC:]
    last = near(7, r.small_out, r.small_back)
    last.start()
    for copy in sides:
        copy.wait()
    states_out[section] = r.states[section]
    states_out[1 - section] = r.states_in[...]
    grads_out[section] = r.grads[section]
    grads_out[1 - section] = r.grads_in[...].astype(F32)
    last.wait()
    row_at = lax.broadcasted_iota(jnp.int32, (16, 128), 0)
    summed = lax.broadcasted_iota(jnp.int32, (16, 128), 1) >= 72
    value = r.small_out[...] + jnp.where(summed, r.small_back[...], 0.0)
    vectors_out[...] = jnp.sum(jnp.where(row_at == me, value, 0.0), axis=0, keepdims=True)


def rotary_tables(places):
    lane = np.arange(128) % HD
    rates = jnp.asarray(np.where(lane < ROT, 10000.0 ** (-2.0 * (lane % (ROT // 2)) / ROT), 0.0), F32)
    angles = places.astype(F32)[:, None] * rates[None, :]
    sine = jnp.sin(angles)
    front = jnp.where(jnp.asarray(lane < ROT // 2), -sine, 0.0)
    back = jnp.where(jnp.asarray((lane >= ROT // 2) & (lane < ROT)), sine, 0.0)
    return jnp.stack([jnp.cos(angles), front, back])


def local(
    block_input,
    out_cotangent,
    segments,
    positions,
    norm_gains,
    norm_shifts,
    inward_weight,
    inward_bias,
    outward_weight,
    outward_bias,
    expand_weight,
    expand_bias,
    shrink_weight,
    shrink_bias,
):
    section = lax.axis_index("section")
    me = lax.axis_index("tensor")
    labels = lax.dynamic_index_in_dim(segments, section, 0, keepdims=False)
    places = lax.dynamic_index_in_dim(positions, section, 0, keepdims=False)
    small = jnp.concatenate(
        [
            inward_bias.reshape(-1),
            expand_bias.reshape(-1),
            outward_bias.reshape(-1),
            shrink_bias.reshape(-1),
            norm_gains.reshape(-1),
            norm_shifts.reshape(-1),
            jnp.zeros((24,), BF),
        ]
    )
    small = jnp.where(jnp.arange(16)[:, None] == me, small[None, :], BF(0))
    pack = jnp.concatenate(
        [inward_weight[0].reshape(16, 768), outward_weight[0].T, expand_weight[0], shrink_weight[0].T, small], axis=1
    )
    vmem = pl.BlockSpec(memory_space=pltpu.VMEM)
    anywhere = pl.BlockSpec(memory_space=pl.ANY)
    dma = pltpu.SemaphoreType.DMA
    states, grads, weights, vectors = pl.pallas_call(
        kernel,
        out_shape=(
            jax.ShapeDtypeStruct((2, OWN, D), BF),
            jax.ShapeDtypeStruct((2, OWN, D), F32),
            jax.ShapeDtypeStruct((16, VEC), F32),
            jax.ShapeDtypeStruct((1, 128), F32),
        ),
        in_specs=[vmem, anywhere, anywhere, vmem, vmem, vmem],
        out_specs=(vmem,) * 4,
        scratch_shapes=[pltpu.VMEM(shape, kind) for shape, kind in SCRATCH.values()]
        + [dma((3, 3, 4)), dma((3, 3, 4)), dma((3, 3, 4)), dma((3, 3, 4)), dma((10,)), dma((10,)), dma((2,))]
        + reduce_scratch(),
        compiler_params=pltpu.CompilerParams(collective_id=0, has_side_effects=True, vmem_limit_bytes=62 << 20),
    )(pack, block_input, out_cotangent, rotary_tables(places), labels[None, :], labels[:, None])
    vec = vectors[0]
    return (
        states[None],
        grads[None],
        vec[72:88].reshape(1, 2, 8),
        vec[88:104].reshape(1, 2, 8),
        weights[:, IN:OUT].reshape(1, 16, 3, 256),
        vec[0:24].reshape(1, 3, 4, 2),
        weights[:, OUT:EXP].T[None],
        vec[56:64].reshape(1, 8),
        weights[:, EXP:SHR][None],
        vec[24:56].reshape(1, 8, 4),
        weights[:, SHR:VEC].T[None],
        vec[64:72].reshape(1, 8),
    )


def solution(mesh):
    return jax.shard_map(
        local,
        mesh=mesh,
        in_specs=(
            P(None, ("dp", "tensor"), None),
            P(None, ("dp", "tensor"), None),
            P(None, "dp"),
            P(None, "dp"),
            P("section", None, ("dp", "tensor")),
            P("section", None, ("dp", "tensor")),
            P("section", "dp", None, "tensor"),
            P("section", None, "tensor", "dp"),
            P("section", "tensor", "dp"),
            P("section", ("dp", "tensor")),
            P("section", "dp", "tensor"),
            P("section", "tensor", "dp"),
            P("section", "tensor", "dp"),
            P("section", ("dp", "tensor")),
        ),
        out_specs=(
            P("section", None, ("dp", "tensor"), None),
            P("section", None, ("dp", "tensor"), None),
            P("section", None, ("dp", "tensor")),
            P("section", None, ("dp", "tensor")),
            P("section", "dp", None, "tensor"),
            P("section", None, "tensor", "dp"),
            P("section", "tensor", "dp"),
            P("section", ("dp", "tensor")),
            P("section", "dp", "tensor"),
            P("section", "tensor", "dp"),
            P("section", "tensor", "dp"),
            P("section", ("dp", "tensor")),
        ),
        check_vma=False,
    )
```

```python
import jax
import jax.numpy as jnp
import numpy as np
from jax import lax
from jax.experimental import pallas as pl
from jax.experimental.pallas import tpu as pltpu
from jax.sharding import PartitionSpec as P

MESH = pl.DeviceIdType.MESH
BF = jnp.bfloat16
F32 = jnp.float32
HD = 64
ROT = 16
LEN = 512
D = 512
OWN = 256
HEADS = 4
EPSILON = 1e-05
MASKED = -1e30

COLS = 3200
VEC, IN, OUT, EXP, SHR = 0, 128, 896, 1152, 2176

GATHER = ((("y", "z", "x"), 0, 1024), (("z", "x", "y"), 1024, 1024), (("x", "y", "z"), 2048, 1152))
REDUCE = ((("x", "z", "y"), 0, 1280), (("z", "x", "y"), 1280, 1280), (("y", "x", "z"), 2560, 640))

V_IN, V_EXP, V_OUTB, V_SHRB, V_G0, V_G1, V_B0, V_B1, V_ALL = 0, 768, 1792, 2304, 2816, 3328, 3840, 4352, 4864


def where_am_i():
    s = lax.axis_index("section")
    d = lax.axis_index("dp")
    return {"x": d % 4, "z": (d // 4) % 4, "y": (d // 16) * 2 + s}


def chip_id(c):
    return {"section": c["y"] % 2, "dp": (c["y"] // 2) * 16 + c["z"] * 4 + c["x"]}


def moved(c, axis, by):
    return {**c, axis: (c[axis] + by) % 4}


def slots(c, free):
    full = slice(None)
    y = c["y"]
    return ((full, full) if "y" in free else (y % 2, y // 2)) + (
        full if "z" in free else c["z"],
        full if "x" in free else c["x"],
    )


def region(ref, c, free, lo, width):
    return ref.at[slots(c, free) + (slice(None), pl.ds(lo, width))]


def greet(c):
    barrier = pltpu.get_barrier_semaphore()
    for axis in "xyz":
        for by in (1, 2, 3):
            pl.semaphore_signal(barrier, inc=1, device_id=chip_id(moved(c, axis, by)), device_id_type=MESH)
    pl.semaphore_signal(barrier, inc=1, device_id={"tensor": 1 - lax.axis_index("tensor")}, device_id_type=MESH)
    pl.semaphore_wait(barrier, 10)


def push(src, dst, send, recv, target):
    return pltpu.make_async_remote_copy(
        src_ref=src, dst_ref=dst, send_sem=send, recv_sem=recv, device_id=target, device_id_type=MESH
    )


def halves(lo, width):
    first = width // 256 * 128
    return (lo, first), (lo + first, width - first)


class Links:
    def __init__(self, send, recv):
        self.send, self.recv, self.started = send, recv, []

    def go(self, src, dst, at, target):
        copy = push(src, dst, self.send.at[at], self.recv.at[at], chip_id(target))
        copy.start()
        self.started.append(copy)

    def arrived(self, dst, at, source):
        push(dst, dst, self.send.at[at], self.recv.at[at], chip_id(source)).wait_recv()

    def close(self):
        for copy in self.started:
            copy.wait_send()


def gather(held, c, links, meanwhile):
    def spot(p, source, by):
        (_, second, _), lo, width = GATHER[p]
        return region(held, moved(source, second, -by), GATHER[p][0][:1], lo, width)

    def part_of(p, source, by, k):
        (_, second, _), lo, width = GATHER[p]
        return region(held, moved(source, second, -by), GATHER[p][0][:1], *halves(lo, width)[k])

    def send_group(p, at, by):
        for k, way in enumerate((1, 3)):
            to = moved(c, GATHER[p][0][2], way)
            for half in (k, 1 - k):
                src = part_of(p, c, by, half)
                links.go(src, src, (p, 6 + 6 * at + 3 * k + (half != k)), to)

    def forward_group(p, at, by):
        for k, way in enumerate((1, 3)):
            third = GATHER[p][0][2]
            source = moved(c, third, -way)
            src = part_of(p, source, by, k)
            links.arrived(src, (p, 6 + 6 * at + 3 * k), source)
            links.go(src, src, (p, 6 + 6 * at + 3 * k + 2), moved(c, third, way))

    for p, (axes, lo, width) in enumerate(GATHER):
        src = region(held, c, (), lo, width)
        for by in (1, 3, 2):
            links.go(src, src, (p, by - 1), moved(c, axes[0], by))
    meanwhile()
    for p, (axes, lo, width) in enumerate(GATHER):
        for by in (1, 3, 2):
            source = moved(c, axes[0], -by)
            links.arrived(region(held, source, (), lo, width), (p, by - 1), source)
        src = spot(p, c, 0)
        for by in (1, 3, 2):
            links.go(src, src, (p, 2 + by), moved(c, axes[1], by))
    for p in range(3):
        send_group(p, 0, 0)
    order = (0, 1, 3, 2)
    for at in range(1, 4):
        by = order[at]
        for p, (axes, lo, width) in enumerate(GATHER):
            links.arrived(spot(p, c, by), (p, 2 + by), moved(c, axes[1], -by))
            send_group(p, at, by)
        for p in range(3):
            forward_group(p, at - 1, order[at - 1])
    for p in range(3):
        forward_group(p, 3, order[3])
    for at, by in enumerate(order):
        for p, (axes, lo, width) in enumerate(GATHER):
            for k, way in enumerate((1, 3)):
                source, far = moved(c, axes[2], -way), moved(c, axes[2], 2)
                links.arrived(part_of(p, source, by, 1 - k), (p, 6 + 6 * at + 3 * k + 1), source)
                links.arrived(part_of(p, far, by, k), (p, 6 + 6 * at + 3 * k + 2), far)


def add_to(target, terms):
    lead = target.shape[:-2]
    for i in range(int(np.prod(lead))):
        at = tuple(int(k) for k in np.unravel_index(i, lead)) if lead else ()
        value = target[at + (...,)].astype(F32)
        for term in terms:
            value = value + term[at + (...,)].astype(F32)
        target[at + (...,)] = value.astype(BF)


def reduce_shapes():
    shapes = []
    for axes, lo, width in REDUCE:
        groups, last = ((8,), (2,)) if axes[2] == "y" else ((4,), (4,))
        rest = (2, 2) if axes[2] == "y" else (4,)
        shapes += [groups + last + (16, halves(lo, width)[k][1]) for k in range(2)]
        shapes += [groups + last + (16, width)] * 2 + [(3,) + rest + (16, width), (3, 16, width)]
    return shapes


class Reduction:
    order = (2, 1, 3, 0)

    def __init__(self, total, c, bufs, links):
        self.total, self.c, self.bufs, self.links = total, c, bufs, links

    def part(self, p, chip, by, layer, k=None):
        axes, lo, width = REDUCE[p]
        chip = moved(chip, axes[1], by)
        lo, width = (lo, width) if k is None else halves(lo, width)[k]
        if layer is None:
            return region(self.total, chip, axes[2:], lo, width)
        return self.total.at[layer, slice(None), chip["z"], chip["x"], slice(None), pl.ds(lo, width)]

    def at(self, by, layer):
        return self.order.index(by) + 4 * (layer or 0)

    def landing(self, p, by, layer, k, half):
        lo, width = REDUCE[p][1:]
        start, size = halves(lo, width)[half]
        return self.bufs[6 * p + 2 + k].at[self.at(by, layer), :, :, pl.ds(start - lo, size)]

    def open(self, p, layer=None):
        c, axis, links = self.c, REDUCE[p][0][0], self.links
        for by in self.order:
            at = self.at(by, layer)
            for k, way in enumerate((1, 3)):
                to = moved(c, axis, way)
                links.go(self.part(p, moved(c, axis, 2), by, layer, k), self.bufs[6 * p + k].at[at], (p, 6 * at + 3 * k), to)
                links.go(self.part(p, to, by, layer, 1 - k), self.landing(p, by, layer, k, 1 - k), (p, 6 * at + 3 * k + 1), to)

    def middle(self, p, by, layer=None):
        c, axis, links = self.c, REDUCE[p][0][0], self.links
        at = self.at(by, layer)
        for k, way in enumerate((1, 3)):
            to = moved(c, axis, way)
            half = self.bufs[6 * p + k].at[at]
            links.arrived(half, (p, 6 * at + 3 * k), moved(c, axis, -way))
            mine = self.part(p, to, by, layer, k)
            add_to(mine, [half])
            links.go(mine, self.landing(p, by, layer, k, k), (p, 6 * at + 3 * k + 2), to)

    def end(self, p, by, layer=None):
        c, axis, links = self.c, REDUCE[p][0][0], self.links
        at = self.at(by, layer)
        for k, way in enumerate((1, 3)):
            for j, half in ((1, 1 - k), (2, k)):
                links.arrived(self.landing(p, by, layer, k, half), (p, 6 * at + 3 * k + j), moved(c, axis, -way))
        add_to(self.part(p, c, by, layer), [self.bufs[6 * p + 2 + k].at[at] for k in range(2)])

    def second(self, p, by):
        axes, lo, width = REDUCE[p]
        to = moved(self.c, axes[1], by)
        self.links.go(region(self.total, to, axes[2:], lo, width), self.bufs[6 * p + 4].at[by - 1], (p, 47 + by), to)

    def third(self, p):
        axes, lo, width = REDUCE[p]
        terms = [self.bufs[6 * p + 4].at[by - 1] for by in (1, 2, 3)]
        for by in (1, 3, 2):
            self.links.arrived(terms[by - 1], (p, 47 + by), moved(self.c, axes[1], -by))
        add_to(region(self.total, self.c, axes[2:], lo, width), terms)
        for by in (1, 3, 2):
            to = moved(self.c, axes[2], by)
            self.links.go(region(self.total, to, (), lo, width), self.bufs[6 * p + 5].at[by - 1], (p, 50 + by), to)

    def last(self, p):
        axes, lo, width = REDUCE[p]
        terms = [self.bufs[6 * p + 5].at[by - 1] for by in (1, 2, 3)]
        for by in (1, 3, 2):
            self.links.arrived(terms[by - 1], (p, 50 + by), moved(self.c, axes[2], -by))
        add_to(region(self.total, self.c, (), lo, width), terms)


def dot(a, b):
    return jnp.dot(a, b, preferred_element_type=F32)


def dot_nt(a, b):
    return lax.dot_general(a, b, (((1,), (1,)), ((), ())), preferred_element_type=F32)


def weight(held, layer, lo, width):
    return held[layer, :, :, :, :, lo : lo + width].reshape(D, width)


def keep_grad(total, layer, lo, value):
    width = value.shape[-1]
    total[layer, :, :, :, :, lo : lo + width] = value.astype(BF).reshape(2, 4, 4, 16, width)


def vector_maps():
    at = lax.broadcasted_iota(jnp.int32, (1, V_ALL), 1)
    exp_at = at - V_EXP
    wide = at - V_OUTB
    is_in, is_exp = at < V_EXP, at < V_OUTB
    owner = jnp.where(is_in, (at & 63) >> 1, jnp.where(is_exp, (exp_at & 127) >> 2, (wide & 511) >> 4))
    row = jnp.where(is_in, ((at >> 8) << 1) + (at & 1), jnp.where(is_exp, 6 + (exp_at & 3), 10 + (wide >> 9)))
    lane = jnp.where(is_in, (at >> 6) & 3, jnp.where(is_exp, exp_at >> 7, wide & 15))
    return owner, row, lane


ROWS = [(k // 2 * 256, 256) for k in range(6)] + [(V_EXP, 1024)] * 4 + [(V_OUTB + D * k, D) for k in range(6)]


def decode_vectors(held, layer, table):
    owner, row, _ = vector_maps()
    block = held[layer, :, :, :, :, VEC:IN].reshape(32, 16, 128).astype(F32)
    owners = lax.broadcasted_iota(jnp.int32, (32, V_ALL), 0)
    pieces = {}
    for k, (lo, width) in enumerate(ROWS):
        spread = dot(block[:, k, :].astype(BF), table[:, lo : lo + width])
        wanted = jnp.where(row == k, owner, -1)[:, lo : lo + width]
        piece = jnp.sum(jnp.where(owners[:, lo : lo + width] == wanted, spread, 0.0), axis=0, keepdims=True)
        pieces[lo] = piece + pieces[lo] if lo in pieces else piece
    return jnp.concatenate(list(pieces.values()), axis=1)


def encode_vectors(total, layer, me, table, vectors):
    owner, row, lane = vector_maps()
    at = lax.broadcasted_iota(jnp.int32, (1, V_ALL), 1)
    source = jnp.where((at >= V_OUTB) & (at < V_G0), lane >> 3, me)
    owner = jnp.where(source == me, owner, -1)
    owners = lax.broadcasted_iota(jnp.int32, (32, V_ALL), 0)
    rows = []
    for k, (lo, width) in enumerate(ROWS):
        wanted = jnp.where(row == k, owner, -1)[:, lo : lo + width]
        chosen = jnp.where(owners[:, lo : lo + width] == wanted, vectors[:, lo : lo + width], 0.0).astype(BF)
        rows.append(dot_nt(chosen, table[:, lo : lo + width])[:, None, :])
    total[layer, :, :, :, :, VEC:IN] = jnp.concatenate(rows, axis=1).astype(BF).reshape(2, 4, 4, 16, 128)


def rolled(values, by):
    return pltpu.roll(values, by % values.shape[-1], 1)


def turned(values, cosine, sine_front, sine_back):
    return values * cosine + rolled(values, -(ROT // 2)) * sine_front + rolled(values, ROT // 2) * sine_back


def rows_of(i):
    return pl.ds(pl.multiple_of(i * OWN, OWN), OWN)


def project(layer, r, i):
    held, vec = r.held, r.vec
    rows = rows_of(i)
    x = r.x[layer, rows, :].astype(F32)
    middle = jnp.mean(x, axis=-1, keepdims=True)
    center = x - middle
    scale = lax.rsqrt(jnp.mean(center * center, axis=-1, keepdims=True) + EPSILON)
    normal = center * scale
    r.moments[layer, 0, rows, :] = jnp.broadcast_to(middle, (OWN, 128))
    r.moments[layer, 1, rows, :] = jnp.broadcast_to(scale, (OWN, 128))
    first = (normal * vec[layer, :, V_G0:V_G1] + vec[layer, :, V_B0:V_B1]).astype(BF)
    second = (normal * vec[layer, :, V_G1:V_B0] + vec[layer, :, V_B1:V_ALL]).astype(BF)
    r.second[rows, :] = second
    r.first_t[layer, :, rows] = first.T
    r.second_t[layer, :, rows] = second.T
    joint = dot(first, weight(held, layer, IN, 768)) + vec[layer, :, V_IN:V_EXP]
    cosine, front, back = [jnp.concatenate([r.angles[k, rows, :]] * 2, axis=1) for k in range(3)]
    query = turned(joint[:, :256], cosine, front, back).astype(BF) * BF(HD**-0.5)
    key = turned(joint[:, 256:512], cosine, front, back).astype(BF)
    value = joint[:, 512:].astype(BF)
    for k, part in enumerate((query, key, value)):
        part_t = part.T
        for h in range(HEADS):
            r.qkv[layer, k, h, rows, :] = part[:, h * HD : (h + 1) * HD]
            r.qkv_t[layer, k, h, :, rows] = part_t[h * HD : (h + 1) * HD]


def attend(layer, r, h):
    for b in range(2):
        keys = (b + 1) * OWN
        cols = slice(b * OWN, keys)
        scores = dot(r.qkv[layer, 1, h, :keys, :], r.qkv_t[layer, 0, h, :, cols]) + r.mask[:keys, cols]
        powers = jnp.exp(scores - jnp.max(scores, axis=0, keepdims=True))
        shares = (powers * (1.0 / jnp.sum(powers, axis=0, keepdims=True))).astype(BF)
        r.shares[layer, h, :keys, cols] = shares
        r.mixed_t[layer, h, :, cols] = dot(r.qkv_t[layer, 2, h, :, :keys], shares)


def widen(layer, r, i):
    rows = rows_of(i)
    before = dot(r.second[rows, :], weight(r.held, layer, EXP, 1024)) + r.vec[layer, :, V_EXP:V_OUTB]
    chance = 0.5 * (1.0 + lax.erf(before * (0.5**0.5)))
    r.hidden[layer, rows, :] = (before * chance).astype(BF)
    slope = chance + before * jnp.exp(-0.5 * before * before) * ((2.0 * np.pi) ** -0.5)
    r.slope[layer, rows, :] = slope.astype(BF)


def close(layer, r, i):
    rows = rows_of(i)
    branch = dot_nt(r.mixed[layer, rows, :], weight(r.held, layer, OUT, 256))
    branch = branch + dot_nt(r.hidden[layer, rows, :], weight(r.held, layer, SHR, 1024))
    r.away[layer, rows, :] = branch.astype(BF)


def enter(layer, r, i):
    held = r.held
    rows = rows_of(i)
    grad = r.grad[layer, rows, :]
    low = grad.astype(BF)
    r.grad_t[:, rows] = low.T
    mixed_grad = dot(low, weight(held, layer, OUT, 256)).astype(BF)
    mixed_grad_t = mixed_grad.T
    for h in range(HEADS):
        r.mixed_grad[h, rows, :] = mixed_grad[:, h * HD : (h + 1) * HD]
        r.mixed_grad_t[h, :, rows] = mixed_grad_t[h * HD : (h + 1) * HD]
    before = (dot(low, weight(held, layer, SHR, 1024)) * r.slope[layer, rows, :].astype(F32)).astype(BF)
    r.before_grad[rows, :] = before
    r.second_grad[rows, :] = dot_nt(before, weight(held, layer, EXP, 1024))
    return jnp.sum(grad, axis=0, keepdims=True)


def outer_grads(layer, r):
    keep_grad(r.total, layer, OUT, dot(r.grad_t[...], r.mixed[layer]))
    for lo in range(0, 1024, 512):
        keep_grad(r.total, layer, SHR + lo, dot(r.grad_t[...], r.hidden[layer, :, lo : lo + 512]))
        keep_grad(r.total, layer, EXP + lo, dot(r.second_t[layer], r.before_grad[:, lo : lo + 512]))


def attend_back(layer, r, h):
    key_parts, value_parts = [], []
    for b in range(2):
        keys = (b + 1) * OWN
        cols = slice(b * OWN, keys)
        shares = r.shares[layer, h, :keys, cols]
        out_t = r.mixed_grad_t[h, :, cols]
        delta = jnp.sum(out_t.astype(F32) * r.mixed_t[layer, h, :, cols], axis=0, keepdims=True)
        share_grad = dot(r.qkv[layer, 2, h, :keys, :], out_t)
        score_grad = (shares.astype(F32) * (share_grad - delta)).astype(BF)
        r.query_grad_t[h, :, cols] = dot(r.qkv_t[layer, 1, h, :, :keys], score_grad) * (HD**-0.5)
        key_parts.append(dot(score_grad, r.qkv[layer, 0, h, cols, :]))
        value_parts.append(dot(shares, r.mixed_grad[h, cols, :]))
    for k, parts in enumerate((key_parts, value_parts)):
        r.pair_grad[k, h, :OWN, :] = parts[0] + parts[1][:OWN]
        r.pair_grad[k, h, OWN:, :] = parts[1][OWN:]


def join(layer, r, i):
    vec = r.vec
    rows = rows_of(i)
    cosine, front, back = [jnp.concatenate([r.angles[k, rows, :]] * 2, axis=1) for k in range(3)]
    query = r.query_grad_t[:, :, rows].reshape(HEADS * HD, OWN).T
    key = jnp.concatenate([r.pair_grad[0, h, rows, :] for h in range(HEADS)], axis=1)
    value = jnp.concatenate([r.pair_grad[1, h, rows, :] for h in range(HEADS)], axis=1)
    query = turned(query, cosine, -front, -back)
    key = turned(key, cosine, -front, -back)
    joint = jnp.concatenate([query, key, value], axis=1).astype(BF)
    r.joint_grad[rows, :] = joint
    first_grad = dot_nt(joint, weight(r.held, layer, IN, 768))
    second_grad = r.second_grad[rows, :]
    middle, scale = [jnp.concatenate([r.moments[layer, k, rows, :]] * 4, axis=1) for k in range(2)]
    normal = (r.x[layer, rows, :].astype(F32) - middle) * scale
    scaled = first_grad * vec[layer, :, V_G0:V_G1] + second_grad * vec[layer, :, V_G1:V_B0]
    passed = scaled - jnp.mean(scaled, axis=-1, keepdims=True)
    passed = passed - normal * jnp.mean(scaled * normal, axis=-1, keepdims=True)
    r.away[3 - layer, rows, :] = (passed * scale).astype(BF)
    terms = [joint.astype(F32), r.before_grad[rows, :].astype(F32)]
    terms += [first_grad * normal, second_grad * normal, first_grad, second_grad]
    return [jnp.sum(term, axis=0, keepdims=True) for term in terms]


def inner_grads(layer, r, out_sum, sums):
    keep_grad(r.total, layer, IN, dot(r.first_t[layer], r.joint_grad[...]))
    vectors = jnp.concatenate([sums[0], sums[1], out_sum, out_sum, *sums[2:]], axis=1)
    encode_vectors(r.total, layer, r.me, r.table, vectors)


class Refs:
    pass


SCRATCH = dict(
    held=((2, 2, 4, 4, 16, COLS), BF),
    total=((2, 2, 4, 4, 16, COLS), BF),
    vec=((2, 1, V_ALL), F32),
    table=((128, V_ALL), BF),
    x=((2, LEN, D), BF),
    cot=((LEN, D), BF),
    grad=((2, LEN, D), F32),
    moments=((2, 2, LEN, 128), F32),
    first_t=((2, D, LEN), BF),
    second_t=((2, D, LEN), BF),
    qkv=((2, 3, HEADS, LEN, HD), BF),
    qkv_t=((2, 3, HEADS, HD, LEN), BF),
    shares=((2, HEADS, LEN, LEN), BF),
    mixed_t=((2, HEADS, HD, LEN), F32),
    mixed=((2, LEN, HEADS * HD), BF),
    hidden=((2, LEN, 1024), BF),
    slope=((2, LEN, 1024), BF),
    mask=((LEN, LEN), F32),
    angles=((3, LEN, 128), F32),
    away=((4, LEN, D), BF),
    come=((4, LEN, D), BF),
    second=((LEN, D), BF),
    grad_t=((D, LEN), BF),
    mixed_grad=((HEADS, LEN, HD), BF),
    mixed_grad_t=((HEADS, HD, LEN), BF),
    before_grad=((LEN, 1024), BF),
    second_grad=((LEN, D), F32),
    query_grad_t=((HEADS, HD, LEN), F32),
    pair_grad=((2, HEADS, LEN, HD), F32),
    joint_grad=((LEN, 768), BF),
    states=((2, OWN, D), BF),
    grads=((2, OWN, D), F32),
    grads_low=((2, OWN, D), BF),
    states_in=((OWN, D), BF),
    grads_in=((OWN, D), BF),
    small=((16, 128), F32),
    small_in=((16, 128), F32),
    small_out=((16, 128), F32),
    small_back=((16, 128), F32),
)


def rotary_tables(angles, r):
    lane = lax.broadcasted_iota(jnp.int32, (1, 128), 1) & (HD - 1)
    rates = jnp.zeros((1, 128), F32)
    for j in range(ROT // 2):
        rates = jnp.where((lane < ROT) & ((lane & 7) == j), 10000.0 ** (-2.0 * j / ROT), rates)
    angles = angles * rates
    sine = jnp.sin(angles)
    r.angles[0] = jnp.cos(angles)
    r.angles[1] = jnp.where(lane < ROT // 2, -sine, 0.0)
    r.angles[2] = jnp.where((lane >= ROT // 2) & (lane < ROT), sine, 0.0)


def kernel(inward, inward_b, outward, outward_b, expand, expand_b, shrink, shrink_b, gains, shifts, *rest):
    x_in, cot_in, labels, places, states_out, grads_out, weights_out, vectors_out, *scratch = rest
    r = Refs()
    names = list(SCRATCH)
    for name, ref in zip(names, scratch):
        setattr(r, name, ref)
    gather_send, gather_recv, reduce_send, reduce_recv, near_send, near_recv, own_sem = scratch[len(names) : len(names) + 7]
    bufs = scratch[len(names) + 7 :]
    c = where_am_i()
    section = lax.axis_index("section")
    me = r.me = lax.axis_index("tensor")
    other = {"tensor": 1 - me}
    mine, theirs = rows_of(me), rows_of(1 - me)

    def near(k, src, dst):
        return push(src, dst, near_send.at[k], near_recv.at[k], other)

    def side(k, src, dst):
        return push(src, dst, near_send.at[k], near_recv.at[k], {"section": 1 - section})

    greet(c)
    held = r.held
    own_slot = slots(c, ())
    small = r.small
    small[...] = jnp.zeros((16, 128), F32)
    for j in range(3):
        small[2 * j : 2 * j + 2, :HEADS] = inward_b[0, j].astype(F32)
    small[6:10, :8] = expand_b[0].astype(F32)
    for t in range(2):
        for at, part in ((10, outward_b[...]), (11, shrink_b[...]), (12, gains[0]), (14, shifts[0])):
            small[at : at + part.shape[0], 8 * t : 8 * t + 8] = jnp.where(me == t, part.astype(F32), 0.0)
    first = near(0, small, r.small_in)
    first.start()

    def pack(lo, value):
        held[own_slot + (slice(None), slice(lo, lo + value.shape[-1]))] = value

    for j in range(3):
        pack(IN + 256 * j, inward[0, j])
    pack(OUT, outward[0])
    pack(EXP, expand[0])
    pack(SHR, shrink[0])
    first.wait()
    row_at = lax.broadcasted_iota(jnp.int32, (16, 128), 0)
    pack(VEC, (small[...] + jnp.where(row_at >= 10, r.small_in[...], 0.0)).astype(BF))
    pairs = [near(1, x_in.at[section], r.x.at[0, mine]), near(2, cot_in.at[section], r.cot.at[mine])]
    owns = [
        pltpu.make_async_copy(x_in.at[section], r.x.at[0, mine], own_sem.at[0]),
        pltpu.make_async_copy(cot_in.at[section], r.cot.at[mine], own_sem.at[1]),
    ]

    def meanwhile():
        for copy in pairs + owns:
            copy.start()
        _, _, lane = vector_maps()
        r.table[...] = (lax.broadcasted_iota(jnp.int32, (128, V_ALL), 0) == lane).astype(F32).astype(BF)

    links = Links(gather_send, gather_recv)
    gather(held, c, links, meanwhile)
    label = labels[pl.ds(section, 1), :].astype(F32)
    place = places[pl.ds(section, 1), :].astype(F32)
    rotary_tables(jnp.broadcast_to(place, (128, LEN)).T, r)
    label_t = jnp.concatenate([jnp.broadcast_to(label, (128, LEN)).T] * 4, axis=1)
    key_at = lax.broadcasted_iota(jnp.int32, (LEN, LEN), 0)
    query_at = lax.broadcasted_iota(jnp.int32, (LEN, LEN), 1)
    r.mask[...] = jnp.where((key_at <= query_at) & (label_t == label), 0.0, MASKED)
    for layer in range(2):
        r.vec[layer] = decode_vectors(held, layer, r.table)
    for copy in pairs + owns:
        copy.wait()
    links.close()

    def swap(k, rows, sem):
        copy = near(sem, r.away.at[k, rows], r.come.at[k, rows])
        copy.start()
        return copy

    def finish(layer, rows):
        bias = r.vec[layer, :, V_OUTB:V_SHRB] + r.vec[layer, :, V_SHRB:V_G0]
        both = r.away[layer, rows, :].astype(F32) + r.come[layer, rows, :].astype(F32)
        return (r.x[layer, rows, :].astype(F32) + both + bias).astype(BF)

    halves_of = [slice(0, OWN), slice(OWN, LEN)]
    swaps = []
    for layer in range(2):
        for i in range(2):
            if layer == 1:
                swaps[i].wait()
                r.x[1, halves_of[i], :] = finish(0, halves_of[i])
            project(layer, r, i)
        for h in range(HEADS):
            attend(layer, r, h)
        r.mixed[layer] = r.mixed_t[layer].reshape(HEADS * HD, LEN).T.astype(BF)
        for i in range(2):
            widen(layer, r, i)
            close(layer, r, i)
            if layer == 0:
                swaps.append(swap(0, halves_of[i], 3 + i))
    r.states[0] = finish(0, mine)
    state_swap = swap(1, theirs, 5)

    links = Links(reduce_send, reduce_recv)
    sums_of = Reduction(r.total, c, bufs, links)
    sides = []
    r.grad[1] = r.cot[...].astype(F32)
    for layer in (1, 0):
        out_sum = jnp.zeros((1, D), F32)
        for i in range(2):
            if layer == 0:
                swaps[i].wait()
                rows = halves_of[i]
                both = r.away[2, rows, :].astype(F32) + r.come[2, rows, :].astype(F32)
                r.grad[0, rows, :] = (r.grad[1, rows, :] + both).astype(BF).astype(F32)
            out_sum = out_sum + enter(layer, r, i)
        if layer == 1:
            state_swap.wait()
            r.states[1] = finish(1, mine)
        else:
            both = r.away[2, mine, :].astype(F32) + r.come[2, mine, :].astype(F32)
            r.grads[1] = r.grad[1, mine, :] + both
        outer_grads(layer, r)
        if layer == 0:
            for by in sums_of.order:
                for p in range(2):
                    sums_of.middle(p, by, 1)
        for h in range(HEADS):
            attend_back(layer, r, h)
        sums = None
        swaps = []
        for i in range(2):
            more = join(layer, r, i)
            sums = more if sums is None else [a + b for a, b in zip(sums, more)]
            if layer == 1:
                swaps.append(swap(2, halves_of[i], 6 + i))
        if layer == 0:
            swaps.append(swap(3, theirs, 8))
        inner_grads(layer, r, out_sum, sums)
        if layer == 1:
            for p in range(2):
                sums_of.open(p, 1)
            sides.append(side(9, r.states.at[1 - section], r.states_in))
            sides[0].start()
    sums_of.open(2)
    for p in range(2):
        sums_of.open(p, 0)
    for by in sums_of.order:
        for p in range(2):
            sums_of.end(p, by, 1)
    swaps[0].wait()
    both = r.away[3, mine, :].astype(F32) + r.come[3, mine, :].astype(F32)
    r.grads[0] = r.grad[0, mine, :] + both
    r.grads_low[...] = r.grads[...].astype(BF)
    for by in sums_of.order:
        sums_of.middle(2, by)
        for p in range(2):
            sums_of.middle(p, by, 0)
    states_out[section] = r.states[section]
    grads_out[section] = r.grads[section]
    for by in sums_of.order:
        for p in range(3):
            sums_of.end(p, by, 0 if p < 2 else None)
            if by:
                sums_of.second(p, by)
    sides.append(side(10, r.grads_low.at[1 - section], r.grads_in))
    sides[1].start()
    for p in range(3):
        sums_of.third(p)
    for p in range(3):
        sums_of.last(p)
    own = r.total[own_slot].astype(F32)
    weights_out[...] = own[:, IN:]
    r.small_out[...] = own[:, VEC:IN]
    last = near(11, r.small_out, r.small_back)
    last.start()
    for copy in sides:
        copy.wait()
    states_out[1 - section] = r.states_in[...]
    grads_out[1 - section] = r.grads_in[...].astype(F32)
    links.close()
    last.wait()
    value = r.small_out[...] + jnp.where(row_at >= 12, r.small_back[...], 0.0)
    vectors_out[...] = jnp.where((row_at >= 10) & (me == 0), pltpu.roll(value, 8, 1), value)


def unpack(states, grads, weights, vectors, *rest):
    states_out, grads_out, gains, shifts, inward, inward_b, outward, outward_b, expand, expand_b, shrink, shrink_b = rest
    states_out[0] = states[...]
    grads_out[0] = grads[...]
    for j in range(3):
        inward[0, j] = weights[:, 256 * j : 256 * (j + 1)]
    outward[0] = weights[:, OUT - IN : EXP - IN]
    expand[0] = weights[:, EXP - IN : SHR - IN]
    shrink[0] = weights[:, SHR - IN :]
    for j in range(3):
        inward_b[0, j] = vectors[2 * j : 2 * j + 2, :HEADS]
    expand_b[0] = vectors[6:10, :8]
    outward_b[...] = vectors[10:11, 8:16]
    shrink_b[...] = vectors[11:12, 8:16]
    gains[0] = vectors[12:14, 8:16]
    shifts[0] = vectors[14:16, 8:16]


def local(
    block_input,
    out_cotangent,
    segments,
    positions,
    norm_gains,
    norm_shifts,
    inward_weight,
    inward_bias,
    outward_weight,
    outward_bias,
    expand_weight,
    expand_bias,
    shrink_weight,
    shrink_bias,
):
    swapped = lambda array: jnp.swapaxes(array, -1, -2)
    vmem = pl.BlockSpec(memory_space=pltpu.VMEM)
    anywhere = pl.BlockSpec(memory_space=pl.ANY)
    dma = pltpu.SemaphoreType.DMA
    results = pl.pallas_call(
        kernel,
        out_shape=(
            jax.ShapeDtypeStruct((2, OWN, D), BF),
            jax.ShapeDtypeStruct((2, OWN, D), F32),
            jax.ShapeDtypeStruct((16, COLS - IN), F32),
            jax.ShapeDtypeStruct((16, 128), F32),
        ),
        in_specs=[vmem] * 10 + [anywhere] * 2 + [vmem] * 2,
        out_specs=(vmem,) * 4,
        scratch_shapes=[pltpu.VMEM(shape, kind) for shape, kind in SCRATCH.values()]
        + [dma((3, 30)), dma((3, 30)), dma((3, 54)), dma((3, 54)), dma((12,)), dma((12,)), dma((2,))]
        + [pltpu.VMEM(shape, BF) for shape in reduce_shapes()],
        compiler_params=pltpu.CompilerParams(collective_id=0, has_side_effects=True, vmem_limit_bytes=62 << 20),
    )(
        jnp.swapaxes(inward_weight, 1, 2),
        swapped(inward_bias),
        swapped(outward_weight),
        outward_bias,
        expand_weight,
        swapped(expand_bias),
        swapped(shrink_weight),
        shrink_bias,
        norm_gains,
        norm_shifts,
        block_input,
        out_cotangent,
        segments,
        positions,
    )
    out_shapes = [(1, 2, OWN, D), (1, 2, OWN, D), (1, 2, 8), (1, 2, 8), (1, 3, 16, 256), (1, 3, 2, 4)]
    out_shapes += [(1, 16, 256), (1, 8), (1, 16, 1024), (1, 4, 8), (1, 16, 1024), (1, 8)]
    outs = pl.pallas_call(
        unpack,
        out_shape=tuple(jax.ShapeDtypeStruct(shape, BF if k == 0 else F32) for k, shape in enumerate(out_shapes)),
        in_specs=[vmem] * 4,
        out_specs=(vmem,) * 12,
    )(*results)
    states, grads, gains, shifts, inward, inward_b, outward, outward_b, expand, expand_b, shrink, shrink_b = outs
    inward = jnp.swapaxes(inward, 1, 2)
    outward, shrink, inward_b, expand_b = [swapped(array) for array in (outward, shrink, inward_b, expand_b)]
    return (states, grads, gains, shifts, inward, inward_b, outward, outward_b, expand, expand_b, shrink, shrink_b)


def solution(mesh):
    return jax.shard_map(
        local,
        mesh=mesh,
        in_specs=(
            P(None, ("dp", "tensor"), None),
            P(None, ("dp", "tensor"), None),
            P(None, "dp"),
            P(None, "dp"),
            P("section", None, ("dp", "tensor")),
            P("section", None, ("dp", "tensor")),
            P("section", "dp", None, "tensor"),
            P("section", None, "tensor", "dp"),
            P("section", "tensor", "dp"),
            P("section", ("dp", "tensor")),
            P("section", "dp", "tensor"),
            P("section", "tensor", "dp"),
            P("section", "tensor", "dp"),
            P("section", ("dp", "tensor")),
        ),
        out_specs=(
            P("section", None, ("dp", "tensor"), None),
            P("section", None, ("dp", "tensor"), None),
            P("section", None, ("dp", "tensor")),
            P("section", None, ("dp", "tensor")),
            P("section", "dp", None, "tensor"),
            P("section", None, "tensor", "dp"),
            P("section", "tensor", "dp"),
            P("section", ("dp", "tensor")),
            P("section", "dp", "tensor"),
            P("section", "tensor", "dp"),
            P("section", "tensor", "dp"),
            P("section", ("dp", "tensor")),
        ),
        check_vma=False,
    )
```

```python
import jax
import jax.numpy as jnp
import numpy as np
from jax import lax
from jax.experimental import pallas as pl
from jax.experimental.pallas import tpu as pltpu
from jax.sharding import PartitionSpec as P

MESH = pl.DeviceIdType.MESH
BF = jnp.bfloat16
F32 = jnp.float32
HD = 64
ROT = 16
LEN = 512
D = 512
OWN = 256
HEADS = 4
EPSILON = 1e-05
MASKED = -1e30

COLS = 3200
VEC, IN, OUT, EXP, SHR = 0, 128, 896, 1152, 2176

GATHER = ((("y", "z", "x"), 0, 1024), (("z", "x", "y"), 1024, 1024), (("x", "y", "z"), 2048, 1152))
REDUCE = (
    (("x", "z", "y"), 1024, 1408),
    (("z", "x", "y"), 0, 1024),
    (("y", "x", "z"), 2432, 384),
    (("y", "z", "x"), 2816, 384),
)

V_IN, V_EXP, V_OUTB, V_SHRB, V_G0, V_G1, V_B0, V_B1, V_ALL = 0, 768, 1792, 2304, 2816, 3328, 3840, 4352, 4864


def where_am_i():
    s = lax.axis_index("section")
    d = lax.axis_index("dp")
    return {"x": d % 4, "z": (d // 4) % 4, "y": (d // 16) * 2 + s}


def chip_id(c):
    return {"section": c["y"] % 2, "dp": (c["y"] // 2) * 16 + c["z"] * 4 + c["x"]}


def moved(c, axis, by):
    return {**c, axis: (c[axis] + by) % 4}


def slots(c, free):
    full = slice(None)
    y = c["y"]
    return ((full, full) if "y" in free else (y % 2, y // 2)) + (
        full if "z" in free else c["z"],
        full if "x" in free else c["x"],
    )


def region(ref, c, free, lo, width):
    return ref.at[slots(c, free) + (slice(None), pl.ds(lo, width))]


def greet(c):
    barrier = pltpu.get_barrier_semaphore()
    for axis in "xyz":
        for by in (1, 2, 3):
            pl.semaphore_signal(barrier, inc=1, device_id=chip_id(moved(c, axis, by)), device_id_type=MESH)
    pl.semaphore_signal(barrier, inc=1, device_id={"tensor": 1 - lax.axis_index("tensor")}, device_id_type=MESH)
    pl.semaphore_wait(barrier, 10)


def push(src, dst, send, recv, target):
    return pltpu.make_async_remote_copy(
        src_ref=src, dst_ref=dst, send_sem=send, recv_sem=recv, device_id=target, device_id_type=MESH
    )


def halves(lo, width):
    first = width // 256 * 128
    return (lo, first), (lo + first, width - first)


class Links:
    def __init__(self, send, recv):
        self.send, self.recv, self.started = send, recv, []

    def go(self, src, dst, at, target):
        copy = push(src, dst, self.send.at[at], self.recv.at[at], chip_id(target))
        copy.start()
        self.started.append(copy)

    def arrived(self, dst, at, source):
        push(dst, dst, self.send.at[at], self.recv.at[at], chip_id(source)).wait_recv()

    def close(self):
        for copy in self.started:
            copy.wait_send()


def gather(held, c, links, pack_vectors, meanwhile):
    def spot(p, source, by):
        (_, second, _), lo, width = GATHER[p]
        return region(held, moved(source, second, -by), GATHER[p][0][:1], lo, width)

    def part_of(p, source, by, k):
        (_, second, _), lo, width = GATHER[p]
        return region(held, moved(source, second, -by), GATHER[p][0][:1], *halves(lo, width)[k])

    def send_group(p, at, by):
        for k, way in enumerate((1, 3)):
            to = moved(c, GATHER[p][0][2], way)
            for half in (k, 1 - k):
                src = part_of(p, c, by, half)
                links.go(src, src, (p, 6 + 6 * at + 3 * k + (half != k)), to)

    def forward_group(p, at, by):
        for k, way in enumerate((1, 3)):
            third = GATHER[p][0][2]
            source = moved(c, third, -way)
            src = part_of(p, source, by, k)
            links.arrived(src, (p, 6 + 6 * at + 3 * k), source)
            links.go(src, src, (p, 6 + 6 * at + 3 * k + 2), moved(c, third, way))

    for p, (axes, lo, width) in reversed(list(enumerate(GATHER))):
        if p == 0:
            pack_vectors()
        src = region(held, c, (), lo, width)
        for by in (1, 3, 2):
            links.go(src, src, (p, by - 1), moved(c, axes[0], by))
    meanwhile()
    for p, (axes, lo, width) in enumerate(GATHER):
        for by in (1, 3, 2):
            source = moved(c, axes[0], -by)
            links.arrived(region(held, source, (), lo, width), (p, by - 1), source)
        src = spot(p, c, 0)
        for by in (1, 3, 2):
            links.go(src, src, (p, 2 + by), moved(c, axes[1], by))
    for p in range(3):
        send_group(p, 0, 0)
    order = (0, 1, 3, 2)
    for at in range(1, 4):
        by = order[at]
        for p, (axes, lo, width) in enumerate(GATHER):
            links.arrived(spot(p, c, by), (p, 2 + by), moved(c, axes[1], -by))
            send_group(p, at, by)
        for p in range(3):
            forward_group(p, at - 1, order[at - 1])
    for p in range(3):
        forward_group(p, 3, order[3])
    for at, by in enumerate(order):
        for p, (axes, lo, width) in enumerate(GATHER):
            for k, way in enumerate((1, 3)):
                source, far = moved(c, axes[2], -way), moved(c, axes[2], 2)
                links.arrived(part_of(p, source, by, 1 - k), (p, 6 + 6 * at + 3 * k + 1), source)
                links.arrived(part_of(p, far, by, k), (p, 6 + 6 * at + 3 * k + 2), far)


def add_to(target, terms):
    lead = target.shape[:-2]
    for i in range(int(np.prod(lead))):
        at = tuple(int(k) for k in np.unravel_index(i, lead)) if lead else ()
        value = target[at + (...,)].astype(F32)
        for term in terms:
            value = value + term[at + (...,)].astype(F32)
        target[at + (...,)] = value.astype(BF)


def reduce_shapes():
    shapes = []
    for axes, lo, width in REDUCE:
        groups, last = ((8,), (2,)) if axes[2] == "y" else ((4,), (4,))
        rest = (2, 2) if axes[2] == "y" else (4,)
        shapes += [groups + last + (16, halves(lo, width)[k][1]) for k in range(2)]
        shapes += [groups + last + (16, width)] * 2 + [(3,) + rest + (16, width), (3, 16, width)]
    return shapes


class Reduction:
    order = (2, 1, 3, 0)

    def __init__(self, total, c, bufs, links):
        self.total, self.c, self.bufs, self.links = total, c, bufs, links

    def part(self, p, chip, by, layer, k=None):
        axes, lo, width = REDUCE[p]
        chip = moved(chip, axes[1], by)
        lo, width = (lo, width) if k is None else halves(lo, width)[k]
        if layer is None:
            return region(self.total, chip, axes[2:], lo, width)
        return self.total.at[layer, slice(None), chip["z"], chip["x"], slice(None), pl.ds(lo, width)]

    def at(self, by, layer):
        return self.order.index(by) + 4 * (layer or 0)

    def landing(self, p, by, layer, k, half):
        lo, width = REDUCE[p][1:]
        start, size = halves(lo, width)[half]
        return self.bufs[6 * p + 2 + k].at[self.at(by, layer), :, :, pl.ds(start - lo, size)]

    def open(self, p, layer=None):
        c, axis, links = self.c, REDUCE[p][0][0], self.links
        for by in self.order:
            at = self.at(by, layer)
            for k, way in enumerate((1, 3)):
                to = moved(c, axis, way)
                links.go(self.part(p, moved(c, axis, 2), by, layer, k), self.bufs[6 * p + k].at[at], (p, 6 * at + 3 * k), to)
                links.go(self.part(p, to, by, layer, 1 - k), self.landing(p, by, layer, k, 1 - k), (p, 6 * at + 3 * k + 1), to)

    def middle(self, p, by, layer=None):
        c, axis, links = self.c, REDUCE[p][0][0], self.links
        at = self.at(by, layer)
        for k, way in enumerate((1, 3)):
            to = moved(c, axis, way)
            half = self.bufs[6 * p + k].at[at]
            links.arrived(half, (p, 6 * at + 3 * k), moved(c, axis, -way))
            mine = self.part(p, to, by, layer, k)
            add_to(mine, [half])
            links.go(mine, self.landing(p, by, layer, k, k), (p, 6 * at + 3 * k + 2), to)

    def end(self, p, by, layer=None):
        c, axis, links = self.c, REDUCE[p][0][0], self.links
        at = self.at(by, layer)
        for k, way in enumerate((1, 3)):
            for j, half in ((1, 1 - k), (2, k)):
                links.arrived(self.landing(p, by, layer, k, half), (p, 6 * at + 3 * k + j), moved(c, axis, -way))
        add_to(self.part(p, c, by, layer), [self.bufs[6 * p + 2 + k].at[at] for k in range(2)])

    def second(self, p, by):
        axes, lo, width = REDUCE[p]
        to = moved(self.c, axes[1], by)
        self.links.go(region(self.total, to, axes[2:], lo, width), self.bufs[6 * p + 4].at[by - 1], (p, 47 + by), to)

    def third(self, p):
        axes, lo, width = REDUCE[p]
        terms = [self.bufs[6 * p + 4].at[by - 1] for by in (1, 2, 3)]
        for by in (1, 3, 2):
            self.links.arrived(terms[by - 1], (p, 47 + by), moved(self.c, axes[1], -by))
        add_to(region(self.total, self.c, axes[2:], lo, width), terms)
        for by in (1, 3, 2):
            to = moved(self.c, axes[2], by)
            self.links.go(region(self.total, to, (), lo, width), self.bufs[6 * p + 5].at[by - 1], (p, 50 + by), to)

    def last(self, p):
        axes, lo, width = REDUCE[p]
        terms = [self.bufs[6 * p + 5].at[by - 1] for by in (1, 2, 3)]
        for by in (1, 3, 2):
            self.links.arrived(terms[by - 1], (p, 50 + by), moved(self.c, axes[2], -by))
        add_to(region(self.total, self.c, (), lo, width), terms)


def dot(a, b):
    return jnp.dot(a, b, preferred_element_type=F32)


def dot_nt(a, b):
    return lax.dot_general(a, b, (((1,), (1,)), ((), ())), preferred_element_type=F32)


def weight(held, layer, lo, width):
    return held[layer, :, :, :, :, lo : lo + width].reshape(D, width)


def keep_grad(total, layer, lo, value):
    width = value.shape[-1]
    total[layer, :, :, :, :, lo : lo + width] = value.astype(BF).reshape(2, 4, 4, 16, width)


def vector_maps():
    at = lax.broadcasted_iota(jnp.int32, (1, V_ALL), 1)
    exp_at = at - V_EXP
    wide = at - V_OUTB
    is_in, is_exp = at < V_EXP, at < V_OUTB
    owner = jnp.where(is_in, (at & 63) >> 1, jnp.where(is_exp, (exp_at & 127) >> 2, (wide & 511) >> 4))
    row = jnp.where(is_in, ((at >> 8) << 1) + (at & 1), jnp.where(is_exp, 6 + (exp_at & 3), 10 + (wide >> 9)))
    lane = jnp.where(is_in, (at >> 6) & 3, jnp.where(is_exp, exp_at >> 7, wide & 15))
    return owner, row, lane


ROWS = [(k // 2 * 256, 256) for k in range(6)] + [(V_EXP, 1024)] * 4 + [(V_OUTB + D * k, D) for k in range(6)]


def decode_vectors(held, layer, table):
    owner, row, _ = vector_maps()
    block = held[layer, :, :, :, :, VEC:IN].reshape(32, 16, 128).astype(F32)
    owners = lax.broadcasted_iota(jnp.int32, (32, V_ALL), 0)
    pieces = {}
    for k, (lo, width) in enumerate(ROWS):
        spread = dot(block[:, k, :].astype(BF), table[:, lo : lo + width])
        wanted = jnp.where(row == k, owner, -1)[:, lo : lo + width]
        piece = jnp.sum(jnp.where(owners[:, lo : lo + width] == wanted, spread, 0.0), axis=0, keepdims=True)
        pieces[lo] = piece + pieces[lo] if lo in pieces else piece
    return jnp.concatenate(list(pieces.values()), axis=1)


def encode_vectors(total, layer, me, table, vectors):
    owner, row, lane = vector_maps()
    at = lax.broadcasted_iota(jnp.int32, (1, V_ALL), 1)
    source = jnp.where((at >= V_OUTB) & (at < V_G0), lane >> 3, me)
    owner = jnp.where(source == me, owner, -1)
    owners = lax.broadcasted_iota(jnp.int32, (32, V_ALL), 0)
    rows = []
    for k, (lo, width) in enumerate(ROWS):
        wanted = jnp.where(row == k, owner, -1)[:, lo : lo + width]
        chosen = jnp.where(owners[:, lo : lo + width] == wanted, vectors[:, lo : lo + width], 0.0).astype(BF)
        rows.append(dot_nt(chosen, table[:, lo : lo + width])[:, None, :])
    total[layer, :, :, :, :, VEC:IN] = jnp.concatenate(rows, axis=1).astype(BF).reshape(2, 4, 4, 16, 128)


def rolled(values, by):
    return pltpu.roll(values, by % values.shape[-1], 1)


def turned(values, cosine, sine_front, sine_back):
    return values * cosine + rolled(values, -(ROT // 2)) * sine_front + rolled(values, ROT // 2) * sine_back


def rows_of(i):
    return pl.ds(pl.multiple_of(i * OWN, OWN), OWN)


def project(layer, r, i):
    held, vec = r.held, r.vec
    rows = rows_of(i)
    x = r.x[layer, rows, :].astype(F32)
    middle = jnp.mean(x, axis=-1, keepdims=True)
    center = x - middle
    scale = lax.rsqrt(jnp.mean(center * center, axis=-1, keepdims=True) + EPSILON)
    normal = center * scale
    r.moments[layer, 0, rows, :] = jnp.broadcast_to(middle, (OWN, 128))
    r.moments[layer, 1, rows, :] = jnp.broadcast_to(scale, (OWN, 128))
    first = (normal * vec[layer, :, V_G0:V_G1] + vec[layer, :, V_B0:V_B1]).astype(BF)
    second = (normal * vec[layer, :, V_G1:V_B0] + vec[layer, :, V_B1:V_ALL]).astype(BF)
    r.second[rows, :] = second
    r.first_t[layer, :, rows] = first.T
    r.second_t[layer, :, rows] = second.T
    joint = dot(first, weight(held, layer, IN, 768)) + vec[layer, :, V_IN:V_EXP]
    cosine, front, back = [jnp.concatenate([r.angles[k, rows, :]] * 2, axis=1) for k in range(3)]
    query = turned(joint[:, :256], cosine, front, back).astype(BF) * BF(HD**-0.5)
    key = turned(joint[:, 256:512], cosine, front, back).astype(BF)
    value = joint[:, 512:].astype(BF)
    for k, part in enumerate((query, key, value)):
        part_t = part.T
        for h in range(HEADS):
            r.qkv[layer, k, h, rows, :] = part[:, h * HD : (h + 1) * HD]
            r.qkv_t[layer, k, h, :, rows] = part_t[h * HD : (h + 1) * HD]


def attend(layer, r, h):
    for b in range(2):
        keys = (b + 1) * OWN
        cols = slice(b * OWN, keys)
        scores = dot(r.qkv[layer, 1, h, :keys, :], r.qkv_t[layer, 0, h, :, cols]) + r.mask[:keys, cols]
        powers = jnp.exp(scores - jnp.max(scores, axis=0, keepdims=True))
        shares = (powers * (1.0 / jnp.sum(powers, axis=0, keepdims=True))).astype(BF)
        r.shares[layer, h, :keys, cols] = shares
        r.mixed_t[layer, h, :, cols] = dot(r.qkv_t[layer, 2, h, :, :keys], shares)


def widen(layer, r, i):
    rows = rows_of(i)
    before = dot(r.second[rows, :], weight(r.held, layer, EXP, 1024)) + r.vec[layer, :, V_EXP:V_OUTB]
    chance = 0.5 * (1.0 + lax.erf(before * (0.5**0.5)))
    r.hidden[layer, rows, :] = (before * chance).astype(BF)
    slope = chance + before * jnp.exp(-0.5 * before * before) * ((2.0 * np.pi) ** -0.5)
    r.slope[layer, rows, :] = slope.astype(BF)


def close(layer, r, i):
    rows = rows_of(i)
    branch = dot_nt(r.mixed[layer, rows, :], weight(r.held, layer, OUT, 256))
    branch = branch + dot_nt(r.hidden[layer, rows, :], weight(r.held, layer, SHR, 1024))
    r.away[layer, rows, :] = branch.astype(BF)


def enter(layer, r, i):
    held = r.held
    rows = rows_of(i)
    grad = r.grad[layer, rows, :]
    low = grad.astype(BF)
    r.grad_t[:, rows] = low.T
    mixed_grad = dot(low, weight(held, layer, OUT, 256)).astype(BF)
    mixed_grad_t = mixed_grad.T
    for h in range(HEADS):
        r.mixed_grad[h, rows, :] = mixed_grad[:, h * HD : (h + 1) * HD]
        r.mixed_grad_t[h, :, rows] = mixed_grad_t[h * HD : (h + 1) * HD]
    before = (dot(low, weight(held, layer, SHR, 1024)) * r.slope[layer, rows, :].astype(F32)).astype(BF)
    r.before_grad[rows, :] = before
    r.second_grad[rows, :] = dot_nt(before, weight(held, layer, EXP, 1024))
    return jnp.sum(grad, axis=0, keepdims=True)


def outer_grads(layer, r):
    keep_grad(r.total, layer, OUT, dot(r.grad_t[...], r.mixed[layer]))
    for lo in range(0, 1024, 512):
        keep_grad(r.total, layer, SHR + lo, dot(r.grad_t[...], r.hidden[layer, :, lo : lo + 512]))
        keep_grad(r.total, layer, EXP + lo, dot(r.second_t[layer], r.before_grad[:, lo : lo + 512]))


def attend_back(layer, r, h):
    key_parts, value_parts = [], []
    for b in range(2):
        keys = (b + 1) * OWN
        cols = slice(b * OWN, keys)
        shares = r.shares[layer, h, :keys, cols]
        out_t = r.mixed_grad_t[h, :, cols]
        delta = jnp.sum(out_t.astype(F32) * r.mixed_t[layer, h, :, cols], axis=0, keepdims=True)
        share_grad = dot(r.qkv[layer, 2, h, :keys, :], out_t)
        score_grad = (shares.astype(F32) * (share_grad - delta)).astype(BF)
        r.query_grad_t[h, :, cols] = dot(r.qkv_t[layer, 1, h, :, :keys], score_grad) * (HD**-0.5)
        key_parts.append(dot(score_grad, r.qkv[layer, 0, h, cols, :]))
        value_parts.append(dot(shares, r.mixed_grad[h, cols, :]))
    for k, parts in enumerate((key_parts, value_parts)):
        r.pair_grad[k, h, :OWN, :] = parts[0] + parts[1][:OWN]
        r.pair_grad[k, h, OWN:, :] = parts[1][OWN:]


def join(layer, r, i):
    vec = r.vec
    rows = rows_of(i)
    cosine, front, back = [jnp.concatenate([r.angles[k, rows, :]] * 2, axis=1) for k in range(3)]
    query = r.query_grad_t[:, :, rows].reshape(HEADS * HD, OWN).T
    key = jnp.concatenate([r.pair_grad[0, h, rows, :] for h in range(HEADS)], axis=1)
    value = jnp.concatenate([r.pair_grad[1, h, rows, :] for h in range(HEADS)], axis=1)
    query = turned(query, cosine, -front, -back)
    key = turned(key, cosine, -front, -back)
    joint = jnp.concatenate([query, key, value], axis=1).astype(BF)
    r.joint_grad[rows, :] = joint
    first_grad = dot_nt(joint, weight(r.held, layer, IN, 768))
    second_grad = r.second_grad[rows, :]
    middle, scale = [jnp.concatenate([r.moments[layer, k, rows, :]] * 4, axis=1) for k in range(2)]
    normal = (r.x[layer, rows, :].astype(F32) - middle) * scale
    scaled = first_grad * vec[layer, :, V_G0:V_G1] + second_grad * vec[layer, :, V_G1:V_B0]
    passed = scaled - jnp.mean(scaled, axis=-1, keepdims=True)
    passed = passed - normal * jnp.mean(scaled * normal, axis=-1, keepdims=True)
    r.away[3 - layer, rows, :] = (passed * scale).astype(BF)
    terms = [joint.astype(F32), r.before_grad[rows, :].astype(F32)]
    terms += [first_grad * normal, second_grad * normal, first_grad, second_grad]
    return [jnp.sum(term, axis=0, keepdims=True) for term in terms]


def inner_grads(layer, r, out_sum, sums):
    keep_grad(r.total, layer, IN, dot(r.first_t[layer], r.joint_grad[...]))
    vectors = jnp.concatenate([sums[0], sums[1], out_sum, out_sum, *sums[2:]], axis=1)
    encode_vectors(r.total, layer, r.me, r.table, vectors)


class Refs:
    pass


SCRATCH = dict(
    held=((2, 2, 4, 4, 16, COLS), BF),
    total=((2, 2, 4, 4, 16, COLS), BF),
    vec=((2, 1, V_ALL), F32),
    table=((128, V_ALL), BF),
    x=((2, LEN, D), BF),
    cot=((LEN, D), BF),
    grad=((2, LEN, D), F32),
    moments=((2, 2, LEN, 128), F32),
    first_t=((2, D, LEN), BF),
    second_t=((2, D, LEN), BF),
    qkv=((2, 3, HEADS, LEN, HD), BF),
    qkv_t=((2, 3, HEADS, HD, LEN), BF),
    shares=((2, HEADS, LEN, LEN), BF),
    mixed_t=((2, HEADS, HD, LEN), F32),
    mixed=((2, LEN, HEADS * HD), BF),
    hidden=((2, LEN, 1024), BF),
    slope=((2, LEN, 1024), BF),
    mask=((LEN, LEN), F32),
    angles=((3, LEN, 128), F32),
    away=((4, LEN, D), BF),
    come=((4, LEN, D), BF),
    second=((LEN, D), BF),
    grad_t=((D, LEN), BF),
    mixed_grad=((HEADS, LEN, HD), BF),
    mixed_grad_t=((HEADS, HD, LEN), BF),
    before_grad=((LEN, 1024), BF),
    second_grad=((LEN, D), F32),
    query_grad_t=((HEADS, HD, LEN), F32),
    pair_grad=((2, HEADS, LEN, HD), F32),
    joint_grad=((LEN, 768), BF),
    states=((2, OWN, D), BF),
    grads=((2, OWN, D), F32),
    grads_low=((2, OWN, D), BF),
    states_in=((OWN, D), BF),
    grads_in=((OWN, D), BF),
    small=((16, 128), F32),
    small_in=((16, 128), F32),
    small_out=((16, 128), F32),
    small_back=((16, 128), F32),
)


def rotary_tables(angles, r):
    lane = lax.broadcasted_iota(jnp.int32, (1, 128), 1) & (HD - 1)
    rates = jnp.zeros((1, 128), F32)
    for j in range(ROT // 2):
        rates = jnp.where((lane < ROT) & ((lane & 7) == j), 10000.0 ** (-2.0 * j / ROT), rates)
    angles = angles * rates
    sine = jnp.sin(angles)
    r.angles[0] = jnp.cos(angles)
    r.angles[1] = jnp.where(lane < ROT // 2, -sine, 0.0)
    r.angles[2] = jnp.where((lane >= ROT // 2) & (lane < ROT), sine, 0.0)


def kernel(inward, inward_b, outward, outward_b, expand, expand_b, shrink, shrink_b, gains, shifts, *rest):
    x_in, cot_in, labels, places, states_out, grads_out, weights_out, vectors_out, *scratch = rest
    r = Refs()
    names = list(SCRATCH)
    for name, ref in zip(names, scratch):
        setattr(r, name, ref)
    gather_send, gather_recv, reduce_send, reduce_recv, near_send, near_recv, own_sem = scratch[len(names) : len(names) + 7]
    bufs = scratch[len(names) + 7 :]
    c = where_am_i()
    section = lax.axis_index("section")
    me = r.me = lax.axis_index("tensor")
    other = {"tensor": 1 - me}
    mine, theirs = rows_of(me), rows_of(1 - me)

    def near(k, src, dst):
        return push(src, dst, near_send.at[k], near_recv.at[k], other)

    def side(k, src, dst):
        return push(src, dst, near_send.at[k], near_recv.at[k], {"section": 1 - section})

    greet(c)
    held = r.held
    own_slot = slots(c, ())
    small = r.small
    small[...] = jnp.zeros((16, 128), F32)
    for j in range(3):
        small[2 * j : 2 * j + 2, :HEADS] = inward_b[0, j].astype(F32)
    small[6:10, :8] = expand_b[0].astype(F32)
    for t in range(2):
        for at, part in ((10, outward_b[...]), (11, shrink_b[...]), (12, gains[0]), (14, shifts[0])):
            small[at : at + part.shape[0], 8 * t : 8 * t + 8] = jnp.where(me == t, part.astype(F32), 0.0)
    first = near(0, small, r.small_in)
    first.start()

    def pack(lo, value):
        held[own_slot + (slice(None), slice(lo, lo + value.shape[-1]))] = value

    for j in range(3):
        pack(IN + 256 * j, inward[0, j])
    pack(OUT, outward[0])
    pack(EXP, expand[0])
    pack(SHR, shrink[0])
    row_at = lax.broadcasted_iota(jnp.int32, (16, 128), 0)

    def pack_vectors():
        first.wait()
        pack(VEC, (small[...] + jnp.where(row_at >= 10, r.small_in[...], 0.0)).astype(BF))
    pairs = [near(1, x_in.at[section], r.x.at[0, mine]), near(2, cot_in.at[section], r.cot.at[mine])]
    owns = [
        pltpu.make_async_copy(x_in.at[section], r.x.at[0, mine], own_sem.at[0]),
        pltpu.make_async_copy(cot_in.at[section], r.cot.at[mine], own_sem.at[1]),
    ]

    def meanwhile():
        for copy in pairs + owns:
            copy.start()
        _, _, lane = vector_maps()
        r.table[...] = (lax.broadcasted_iota(jnp.int32, (128, V_ALL), 0) == lane).astype(F32).astype(BF)

        label = labels[pl.ds(section, 1), :].astype(F32)
        place = places[pl.ds(section, 1), :].astype(F32)
        rotary_tables(jnp.broadcast_to(place, (128, LEN)).T, r)
        label_t = jnp.concatenate([jnp.broadcast_to(label, (128, LEN)).T] * 4, axis=1)
        key_at = lax.broadcasted_iota(jnp.int32, (LEN, LEN), 0)
        query_at = lax.broadcasted_iota(jnp.int32, (LEN, LEN), 1)
        r.mask[...] = jnp.where((key_at <= query_at) & (label_t == label), 0.0, MASKED)

    links = Links(gather_send, gather_recv)
    gather(held, c, links, pack_vectors, meanwhile)
    for layer in range(2):
        r.vec[layer] = decode_vectors(held, layer, r.table)
    for copy in pairs + owns:
        copy.wait()
    links.close()

    def swap(k, rows, sem):
        copy = near(sem, r.away.at[k, rows], r.come.at[k, rows])
        copy.start()
        return copy

    def finish(layer, rows):
        bias = r.vec[layer, :, V_OUTB:V_SHRB] + r.vec[layer, :, V_SHRB:V_G0]
        both = r.away[layer, rows, :].astype(F32) + r.come[layer, rows, :].astype(F32)
        return (r.x[layer, rows, :].astype(F32) + both + bias).astype(BF)

    halves_of = [slice(0, OWN), slice(OWN, LEN)]
    swaps = []
    for layer in range(2):
        for i in range(2):
            if layer == 1:
                swaps[i].wait()
                r.x[1, halves_of[i], :] = finish(0, halves_of[i])
            project(layer, r, i)
        for h in range(HEADS):
            attend(layer, r, h)
        r.mixed[layer] = r.mixed_t[layer].reshape(HEADS * HD, LEN).T.astype(BF)
        for i in range(2):
            widen(layer, r, i)
            close(layer, r, i)
            if layer == 0:
                swaps.append(swap(0, halves_of[i], 3 + i))
    r.states[0] = finish(0, mine)
    state_swap = swap(1, theirs, 5)

    links = Links(reduce_send, reduce_recv)
    sums_of = Reduction(r.total, c, bufs, links)
    sides = []
    r.grad[1] = r.cot[...].astype(F32)
    for layer in (1, 0):
        out_sum = jnp.zeros((1, D), F32)
        for i in range(2):
            if layer == 0:
                swaps[i].wait()
                rows = halves_of[i]
                both = r.away[2, rows, :].astype(F32) + r.come[2, rows, :].astype(F32)
                r.grad[0, rows, :] = (r.grad[1, rows, :] + both).astype(BF).astype(F32)
            out_sum = out_sum + enter(layer, r, i)
        if layer == 1:
            state_swap.wait()
            r.states[1] = finish(1, mine)
            sides.append(side(9, r.states.at[1 - section], r.states_in))
            sides[0].start()
        else:
            both = r.away[2, mine, :].astype(F32) + r.come[2, mine, :].astype(F32)
            r.grads[1] = r.grad[1, mine, :] + both
        outer_grads(layer, r)
        if layer == 0:
            for by in sums_of.order:
                sums_of.middle(0, by, 1)
            sums_of.open(2)
            sums_of.open(3)
        sums_of.open(0, layer)
        for h in range(HEADS):
            attend_back(layer, r, h)
        sums = None
        swaps = []
        for i in range(2):
            more = join(layer, r, i)
            sums = more if sums is None else [a + b for a, b in zip(sums, more)]
            if layer == 1:
                swaps.append(swap(2, halves_of[i], 6 + i))
        if layer == 0:
            swaps.append(swap(3, theirs, 8))
        inner_grads(layer, r, out_sum, sums)
        sums_of.open(1, layer)
    for by in sums_of.order:
        sums_of.middle(1, by, 1)
    for by in sums_of.order:
        sums_of.middle(2, by)
        sums_of.middle(3, by)
        sums_of.middle(0, by, 0)
    swaps[0].wait()
    both = r.away[3, mine, :].astype(F32) + r.come[3, mine, :].astype(F32)
    r.grads[0] = r.grad[0, mine, :] + both
    r.grads_low[...] = r.grads[...].astype(BF)
    for by in sums_of.order:
        sums_of.end(0, by, 1)
    for by in sums_of.order:
        sums_of.middle(1, by, 0)
    states_out[section] = r.states[section]
    grads_out[section] = r.grads[section]
    for by in sums_of.order:
        sums_of.end(2, by)
        sums_of.end(3, by)
        sums_of.end(0, by, 0)
        if by:
            for p in (2, 3, 0):
                sums_of.second(p, by)
    for by in sums_of.order:
        sums_of.end(1, by, 1)
        sums_of.end(1, by, 0)
        if by:
            sums_of.second(1, by)
    sides.append(side(10, r.grads_low.at[1 - section], r.grads_in))
    sides[1].start()
    for p in (2, 3, 0, 1):
        sums_of.third(p)
    for p in (2, 3, 0, 1):
        sums_of.last(p)
    own = r.total[own_slot].astype(F32)
    weights_out[...] = own[:, IN:]
    r.small_out[...] = own[:, VEC:IN]
    last = near(11, r.small_out, r.small_back)
    last.start()
    for copy in sides:
        copy.wait()
    states_out[1 - section] = r.states_in[...]
    grads_out[1 - section] = r.grads_in[...].astype(F32)
    links.close()
    last.wait()
    value = r.small_out[...] + jnp.where(row_at >= 12, r.small_back[...], 0.0)
    vectors_out[...] = jnp.where((row_at >= 10) & (me == 0), pltpu.roll(value, 8, 1), value)


def unpack(states, grads, weights, vectors, *rest):
    states_out, grads_out, gains, shifts, inward, inward_b, outward, outward_b, expand, expand_b, shrink, shrink_b = rest
    states_out[0] = states[...]
    grads_out[0] = grads[...]
    for j in range(3):
        inward[0, j] = weights[:, 256 * j : 256 * (j + 1)]
    outward[0] = weights[:, OUT - IN : EXP - IN]
    expand[0] = weights[:, EXP - IN : SHR - IN]
    shrink[0] = weights[:, SHR - IN :]
    for j in range(3):
        inward_b[0, j] = vectors[2 * j : 2 * j + 2, :HEADS]
    expand_b[0] = vectors[6:10, :8]
    outward_b[...] = vectors[10:11, 8:16]
    shrink_b[...] = vectors[11:12, 8:16]
    gains[0] = vectors[12:14, 8:16]
    shifts[0] = vectors[14:16, 8:16]


def local(
    block_input,
    out_cotangent,
    segments,
    positions,
    norm_gains,
    norm_shifts,
    inward_weight,
    inward_bias,
    outward_weight,
    outward_bias,
    expand_weight,
    expand_bias,
    shrink_weight,
    shrink_bias,
):
    swapped = lambda array: jnp.swapaxes(array, -1, -2)
    vmem = pl.BlockSpec(memory_space=pltpu.VMEM)
    anywhere = pl.BlockSpec(memory_space=pl.ANY)
    dma = pltpu.SemaphoreType.DMA
    results = pl.pallas_call(
        kernel,
        out_shape=(
            jax.ShapeDtypeStruct((2, OWN, D), BF),
            jax.ShapeDtypeStruct((2, OWN, D), F32),
            jax.ShapeDtypeStruct((16, COLS - IN), F32),
            jax.ShapeDtypeStruct((16, 128), F32),
        ),
        in_specs=[vmem] * 10 + [anywhere] * 2 + [vmem] * 2,
        out_specs=(vmem,) * 4,
        scratch_shapes=[pltpu.VMEM(shape, kind) for shape, kind in SCRATCH.values()]
        + [dma((3, 30)), dma((3, 30)), dma((4, 54)), dma((4, 54)), dma((12,)), dma((12,)), dma((2,))]
        + [pltpu.VMEM(shape, BF) for shape in reduce_shapes()],
        compiler_params=pltpu.CompilerParams(collective_id=0, has_side_effects=True, vmem_limit_bytes=62 << 20),
    )(
        jnp.swapaxes(inward_weight, 1, 2),
        swapped(inward_bias),
        swapped(outward_weight),
        outward_bias,
        expand_weight,
        swapped(expand_bias),
        swapped(shrink_weight),
        shrink_bias,
        norm_gains,
        norm_shifts,
        block_input,
        out_cotangent,
        segments,
        positions,
    )
    out_shapes = [(1, 2, OWN, D), (1, 2, OWN, D), (1, 2, 8), (1, 2, 8), (1, 3, 16, 256), (1, 3, 2, 4)]
    out_shapes += [(1, 16, 256), (1, 8), (1, 16, 1024), (1, 4, 8), (1, 16, 1024), (1, 8)]
    outs = pl.pallas_call(
        unpack,
        out_shape=tuple(jax.ShapeDtypeStruct(shape, BF if k == 0 else F32) for k, shape in enumerate(out_shapes)),
        in_specs=[vmem] * 4,
        out_specs=(vmem,) * 12,
    )(*results)
    states, grads, gains, shifts, inward, inward_b, outward, outward_b, expand, expand_b, shrink, shrink_b = outs
    inward = jnp.swapaxes(inward, 1, 2)
    outward, shrink, inward_b, expand_b = [swapped(array) for array in (outward, shrink, inward_b, expand_b)]
    return (states, grads, gains, shifts, inward, inward_b, outward, outward_b, expand, expand_b, shrink, shrink_b)


def solution(mesh):
    return jax.shard_map(
        local,
        mesh=mesh,
        in_specs=(
            P(None, ("dp", "tensor"), None),
            P(None, ("dp", "tensor"), None),
            P(None, "dp"),
            P(None, "dp"),
            P("section", None, ("dp", "tensor")),
            P("section", None, ("dp", "tensor")),
            P("section", "dp", None, "tensor"),
            P("section", None, "tensor", "dp"),
            P("section", "tensor", "dp"),
            P("section", ("dp", "tensor")),
            P("section", "dp", "tensor"),
            P("section", "tensor", "dp"),
            P("section", "tensor", "dp"),
            P("section", ("dp", "tensor")),
        ),
        out_specs=(
            P("section", None, ("dp", "tensor"), None),
            P("section", None, ("dp", "tensor"), None),
            P("section", None, ("dp", "tensor")),
            P("section", None, ("dp", "tensor")),
            P("section", "dp", None, "tensor"),
            P("section", None, "tensor", "dp"),
            P("section", "tensor", "dp"),
            P("section", ("dp", "tensor")),
            P("section", "dp", "tensor"),
            P("section", "tensor", "dp"),
            P("section", "tensor", "dp"),
            P("section", ("dp", "tensor")),
        ),
        check_vma=False,
    )
```
